128 devices in a mesh: dp: 16 (over y, x_lo, core), seq: 8 (over x_hi, z).
Axes of the slice: x: 4 (x_hi: 2, x_lo: 2; x = x_hi * 2 + x_lo), y: 4, z: 4, core: 2. Of those that a mesh axis runs over, the one named last changes fastest.
Arguments:
- tokens: bfloat16 [16384, 1280], P(('dp', 'seq')), may hold values from -24 to 24
- teacher: bfloat16 [16384, 1280], P(('dp', 'seq')), may hold values from -20 to 20
- prefix: int32 [16], replicated, may hold values from 1 to 1024
- routes: int32 [16384, 2], P(('dp', 'seq')), may hold values from 0 to 2, all different within a row
- attn_gain: bfloat16 [1280], P(('dp', 'seq')), may hold values from 0.099609375 to 1.8984375
- w_qkv: bfloat16 [1280, 3840], P(('dp', 'seq')), may hold values from -0.15625 to 0.15625
- w_out: bfloat16 [1280, 1280], P(('dp', 'seq')), may hold values from -2 to 2
- router_w: bfloat16 [1280, 3], P(('dp', 'seq')), may hold values from -0.078125 to 0.078125
- ffn_gain: bfloat16 [1280], P(('dp', 'seq')), may hold values from 0.099609375 to 1.8984375
- w_gate_up: bfloat16 [1280, 4, 2, 896], P('dp', None, None, 'seq'), may hold values from -0.15625 to 0.15625
- w_down: bfloat16 [1280, 4, 896], P('dp', None, 'seq'), may hold values from -0.1875 to 0.1875
Outputs:
- activations: bfloat16 [16384, 1280], P(('dp', 'seq'))
- loss: float32 [], replicated
- d_tokens: float32 [16384, 1280], P(('dp', 'seq'))
- d_attn_gain: float32 [1280], P(('dp', 'seq'))
- d_w_qkv: float32 [1280, 3840], P(('dp', 'seq'))
- d_w_out: float32 [1280, 1280], P(('dp', 'seq'))
- d_router_w: float32 [1280, 3], P(('dp', 'seq'))
- d_ffn_gain: float32 [1280], P(('dp', 'seq'))
- d_w_gate_up: float32 [1280, 4, 2, 896], P('dp', None, None, 'seq')
- d_w_down: float32 [1280, 4, 896], P('dp', None, 'seq')
The draws below stay inside these ranges and needn't reach their ends.
Inputs may be any that keep to these rules, and one draw needn't show every extreme that they name: `routes`: each token's 2 routed experts are different.
All inputs are finite; a program needn't handle non-finite values.
Results may differ from the reference program's by a relative error of at most 0.017.
Values may be sent and summed in bfloat16 or wider, within the bound.
No kernel may reach another device: no remote copies, remote signals or barrier semaphores. Data moves between devices by JAX's collectives and lax.ppermute only.
A program may use at most 192 MiB of HBM per device.

```python
import jax
import jax.numpy as jnp
from jax import lax

D = 1280
HEADS = 10
HEAD_DIM = 128
FF = 896
TOP = 2
EXP_R = 3
EXPERTS = 4
SEQ_LEN = 1024
SEQS = 16
TOKENS = 16384


def draw_teacher(key, part):
    places = jnp.arange(TOKENS, dtype=jnp.int32).astype(jnp.float32)[:, None]
    spread = 1.0 + 2.0 * places / max(TOKENS - 1, 1)
    values = jax.random.normal(key, (TOKENS, D), jnp.float32) * spread
    return jnp.clip(values, -20.0, 20.0).astype(jnp.bfloat16)


def plant(entries, key, smallest, top_value):
    place = [jax.random.randint(jax.random.fold_in(key, axis), (), 0, length) for axis, length in enumerate(entries.shape)]
    longest = entries.shape.index(max(entries.shape))
    next_to = place[:longest] + [(place[longest] + 1) % entries.shape[longest]] + place[longest + 1:]
    return entries.at[tuple(place)].set(smallest).at[tuple(next_to)].set(top_value)


def raised(array, rng, source, target, parts, factor):
    def block_of(axis_at):
        return (jnp.arange(array.shape[axis_at]) // (array.shape[axis_at] // parts)).reshape((-1,) + (1,) * (array.ndim - 1 - axis_at))

    near = jax.random.permutation(rng, parts)[block_of(target)]
    far = (block_of(target) + parts // 2) % parts
    return jnp.where((block_of(source) == near) | (block_of(source) == far), factor * array, array)


def level_of(own_key, extent, cuts, smallest, top_value):
    factor_of = 1.0
    for axis_at, shards_of in cuts:
        draws = jax.random.uniform(jax.random.fold_in(jax.random.fold_in(own_key, 6), axis_at), (shards_of,), jnp.float32, smallest / len(cuts), top_value / len(cuts))
        factor_of = factor_of * jnp.repeat(jnp.exp(draws), extent[axis_at] // shards_of).reshape((-1,) + (1,) * (len(extent) - 1 - axis_at))
    return factor_of


def choose_distinct(key, rows, number_of, top, lift):
    ranking = jax.random.permutation(jax.random.fold_in(key, 1), number_of)
    boost = ranking
    for power in range(3):
        boost = boost * boost // number_of
    boost = boost * lift // number_of
    chance = jax.random.randint(jax.random.fold_in(key, 2), (rows, number_of), 0, 4096) + boost
    sure = jax.random.permutation(jax.random.fold_in(key, 3), rows)[jnp.arange(number_of) % rows]
    chance = jnp.where(jnp.arange(rows)[:, None] == sure[None, :], 1 << 14, chance)
    priority = chance * number_of + jnp.arange(number_of)
    return lax.top_k(priority.astype(jnp.int32), top)[1].astype(jnp.int32)


def bell_draw(key, shape, width, bound, cuts=(), kind=jnp.bfloat16):
    values = width * jax.random.normal(key, shape, jnp.float32)
    if cuts:
        values = values * level_of(key, shape, cuts, -0.22, 0.18)
    return jnp.clip(values, -bound, bound).astype(kind)


def noise_with(key, shape, scale, bound, shards, heavy, held_as=jnp.bfloat16):
    array = scale * jax.random.normal(key, shape, jnp.float32)
    if shards:
        array = array * level_of(key, shape, shards, -0.22, 0.18)
    return jnp.clip(raised(array, jax.random.fold_in(key, 3), *heavy), -bound, bound).astype(held_as)


def setup_inputs(seed: int = 0) -> dict:
    key_list = jax.random.split(jax.random.key(seed), 12)
    tokens = noise_with(key_list[0], (TOKENS, D), 1.0, 24.0, ((0, 128),), (0, 1, 128, 5.5))
    teacher = draw_teacher(jax.random.fold_in(key_list[11], 71), 0)
    prefix = plant(jax.random.randint(key_list[2], (SEQS,), 1, SEQ_LEN + 1), jax.random.fold_in(key_list[2], 1), 1, SEQ_LEN).astype(jnp.int32)
    routes = choose_distinct(key_list[3], TOKENS, EXP_R, TOP, 5461)
    attn_gain = jnp.clip(1.0 + 0.18 * jax.random.normal(key_list[4], (D,), jnp.float32), 0.099609375, 1.8984375).astype(jnp.bfloat16)
    w_qkv = bell_draw(key_list[5], (D, 3 * D), D ** -0.5, 0.15625, ((0, 128),))
    w_out = bell_draw(key_list[6], (D, D), (max(1, D * 8 // SEQ_LEN)) ** -0.5, 2.0, ((0, 128),))
    router_w = bell_draw(key_list[7], (D, EXP_R), (4 * D) ** -0.5, 0.078125, ((0, 128),))
    ffn_gain = jnp.clip(1.0 + 0.18 * jax.random.normal(key_list[8], (D,), jnp.float32), 0.099609375, 1.8984375).astype(jnp.bfloat16)
    w_gate_up = bell_draw(key_list[9], (D, EXPERTS, 2, FF), D ** -0.5, 0.15625, ((0, 16), (3, 8)))
    w_down = bell_draw(key_list[10], (D, EXPERTS, FF), FF ** -0.5, 0.1875, ((0, 16), (2, 8)))
    return {"tokens": tokens, "teacher": teacher, "prefix": prefix, "routes": routes, "attn_gain": attn_gain, "w_qkv": w_qkv, "w_out": w_out, "router_w": router_w, "ffn_gain": ffn_gain, "w_gate_up": w_gate_up, "w_down": w_down}


@jax.custom_vjp
def low(v):
    return lax.optimization_barrier(v.astype(jnp.bfloat16)).astype(jnp.float32)

@jax.custom_vjp
def low_back(v):
    return v

def low_keep(v):
    return (low(v), None)

def low_pass(kept, grad):
    return (grad,)

def back_keep(v):
    return (v, None)

def back_low(kept, grad):
    return (low(grad),)
low.defvjp(low_keep, low_pass)
low_back.defvjp(back_keep, back_low)
norm_eps = 1e-06
masked_score = -1e+30
rope_base = 10000.0
highest = lax.Precision.HIGHEST

def normed(values):
    return values * lax.rsqrt(lax.optimization_barrier(jnp.mean(values * values, axis=-1, keepdims=True)) + norm_eps)

def turned(values):
    half_dim = values.shape[-1] // 2
    return jnp.concatenate([-values[..., half_dim:], values[..., :half_dim]], axis=-1)

def rope_tables(count):
    places = jnp.arange(count, dtype=jnp.int32).astype(jnp.float32)
    half_dim = HEAD_DIM // 2
    speeds = rope_base ** (-jnp.arange(half_dim, dtype=jnp.float32) / half_dim)
    angles = places[:, None] * speeds[None, :]
    cosine = jnp.concatenate([jnp.cos(angles), jnp.cos(angles)], axis=-1)[:, None, :]
    sine = jnp.concatenate([jnp.sin(angles), jnp.sin(angles)], axis=-1)[:, None, :]
    return (cosine, sine)

def layer(inputs, attn_gain, w_qkv, w_out, router_w, ffn_gain, w_gate_up, w_down, routes, prefix_len):
    length = inputs.shape[0]
    first_h = low(normed(inputs) * attn_gain)
    qkv = low_back(jnp.dot(first_h, w_qkv, precision=highest))
    cosine, sine = rope_tables(length)
    queries = qkv[:, :D].reshape(length, HEADS, HEAD_DIM)
    key_rows = qkv[:, D:2 * D].reshape(length, HEADS, HEAD_DIM)
    value_rows = low(qkv[:, 2 * D:].reshape(length, HEADS, HEAD_DIM))
    queries = low(queries * cosine + turned(queries) * sine)
    key_rows = low(key_rows * cosine + turned(key_rows) * sine)
    raw = jnp.einsum('thd,shd->hts', queries, key_rows, precision=highest)
    scores = HEAD_DIM ** (-0.5) * low_back(raw)
    places = jnp.arange(length, dtype=jnp.int32)
    visible = (places[None, :] <= places[:, None]) | (places[None, :] < prefix_len)
    scores = jnp.where(visible[None], scores, masked_score)
    probs = jax.nn.softmax(scores, axis=-1)
    mixed = jnp.einsum('hts,shd->thd', low(probs), value_rows, precision=highest).reshape(length, D)
    mixed = low(low_back(mixed))
    attn = low_back(jnp.dot(mixed, w_out.T, precision=highest))
    after_attn = inputs + attn
    second_h = low(normed(after_attn) * ffn_gain)
    logits = low_back(jnp.dot(second_h, router_w, precision=highest))
    gates = jax.nn.softmax(logits, axis=-1)
    chosen = jnp.any(routes[:, :, None] == jnp.arange(EXP_R, dtype=jnp.int32)[None, None, :], axis=1)
    combine = jnp.concatenate([jnp.ones((length, 1), gates.dtype), jnp.where(chosen, gates, 0.0)], axis=1)
    gate_up = low_back(jnp.einsum('td,degf->tegf', second_h, w_gate_up, precision=highest))
    gate_part = gate_up[:, :, 0, :]
    up_part = gate_up[:, :, 1, :]
    hidden = low(combine[:, :, None] * jax.nn.silu(gate_part) * up_part)
    expert_out = low_back(jnp.einsum('tef,def->td', hidden, w_down, precision=highest))
    return after_attn + expert_out

def reference(tokens, teacher, prefix, routes, attn_gain, w_qkv, w_out, router_w, ffn_gain, w_gate_up, w_down):
    weights = tuple((item.astype(jnp.float32) for item in (attn_gain, w_qkv, w_out, router_w, ffn_gain, w_gate_up, w_down)))
    seq_inputs = tokens.astype(jnp.float32).reshape(SEQS, SEQ_LEN, D)
    seq_teacher = teacher.astype(jnp.float32).reshape(SEQS, SEQ_LEN, D)
    seq_routes = routes.reshape(SEQS, SEQ_LEN, TOP)

    def step(carry, item):
        grads, squares = carry
        inputs, target, route_rows, prefix_len = item

        def apply(values, *params):
            return layer(values, *params, route_rows, prefix_len)
        outputs, pull = jax.vjp(apply, inputs, *weights)
        diff = outputs - target
        back = pull(diff)
        grads = tuple((total + piece for total, piece in zip(grads, back[1:])))
        return ((grads, squares + jnp.sum(diff * diff)), (outputs.astype(jnp.bfloat16), back[0]))
    start = (tuple((jnp.zeros_like(item) for item in weights)), jnp.zeros((), jnp.float32))
    (grads, squares), (outs_all, grad_inputs) = lax.scan(step, start, (seq_inputs, seq_teacher, seq_routes, prefix))
    return (outs_all.reshape(TOKENS, D), squares / TOKENS, grad_inputs.reshape(TOKENS, D), grads[0], grads[1], grads[2], grads[3], grads[4], grads[5], grads[6])
```

```python
import functools

import jax
import jax.numpy as jnp
import numpy as np
from jax import lax
from jax.experimental import pallas as pl
from jax.experimental.pallas import tpu as pltpu
from jax.sharding import Mesh, PartitionSpec as P

D = 1280
HD = 128
HEADS = 10
SLOTS = 2
GROUPS = 5
HW = SLOTS * HD
QKV = 3 * HW
EXT = 128
WA = QKV + HW + EXT
ROWS = 128
SEQ = 1024
UNITS = 112
GU = 4 * 2 * 128
DN = 4 * 128
WM = GU + DN
norm_eps = 1e-06
masked_score = -1e30
rope_base = 10000.0
SCALE = HD ** (-0.5)
F32 = jnp.float32
BF16 = jnp.bfloat16
VMEM_LIMIT = 58 * 1024 * 1024

NT = (((1,), (1,)), ((), ()))
TN = (((0,), (0,)), ((), ()))


def dot(a, b):
    return jnp.dot(a, b, preferred_element_type=F32)


def dot_nt(a, b):
    return lax.dot_general(a, b, NT, preferred_element_type=F32)


def rows_of(start, count=ROWS):
    return pl.ds(pl.multiple_of(start, ROWS), count)


def half_turn(u):
    return pltpu.roll(u, HD // 2, 1)


def attn_fwd_kernel(info, *refs):
    xs = refs[:8]
    w, cos, sin = refs[8:11]
    a, b, h1, q, k, v, mixed, lse, ext, chosen = refs[11:21]
    part, vt = refs[21:]
    ext_t = w[:, QKV + HW : WA].astype(F32).T
    ext[...] = ext_t
    gain = ext_t[0:1, :]
    for i in range(8):
        blk = xs[i][:, :D].astype(F32)
        r = lax.rsqrt(jnp.mean(blk * blk, axis=1, keepdims=True) + norm_eps)
        at = rows_of(info[i] * ROWS)
        h1[at, :] = (blk * r * gain).astype(BF16)
        chosen[at, :] = xs[i][:, D:]

    @pl.loop(0, 4)
    def _(step):
        at = rows_of(step * 256, 256)
        full = dot(h1[at, :], w[:, :QKV])
        c, s = cos[at, :], sin[at, :]
        for j in range(SLOTS):
            col = slice(j * HD, (j + 1) * HD)
            u = full[:, j * HD : (j + 1) * HD]
            q[at, col] = (u * c + half_turn(u) * s).astype(BF16)
            u = full[:, HW + j * HD : HW + (j + 1) * HD]
            k[at, col] = (u * c + half_turn(u) * s).astype(BF16)
            u = full[:, 2 * HW + j * HD : 2 * HW + (j + 1) * HD]
            v[at, col] = u.astype(BF16)
            vt[col, at] = u.T.astype(BF16)

    prefix = info[16]
    lse[...] = jnp.zeros_like(lse)
    for j in range(SLOTS):
        col = slice(j * HD, (j + 1) * HD)

        @pl.loop(0, 4)
        def _(step, j=j, col=col):
            at = rows_of(step * 256, 256)
            s = dot_nt(k[:, col], q[at, col]) * SCALE
            key = lax.broadcasted_iota(jnp.int32, (SEQ, 256), 0)
            query = lax.broadcasted_iota(jnp.int32, (SEQ, 256), 1) + step * 256
            s = jnp.where(key < jnp.maximum(query + 1, prefix), s, masked_score)
            top = jnp.max(s, axis=0, keepdims=True)
            e = jnp.exp(s - top)
            total = jnp.sum(e, axis=0, keepdims=True)
            pn = (e * (1.0 / total)).astype(BF16)
            mixed[at, col] = dot(vt[col, :], pn).T.astype(BF16)
            lse[j : j + 1, at] = top + jnp.log(total)

    @pl.loop(0, 4)
    def _(step):
        at = rows_of(step * 256, 256)
        part[at, :] = dot_nt(mixed[at, :], w[:, QKV : QKV + HW]).astype(BF16)

    for i in range(4):
        out = slice(i * ROWS, (i + 1) * ROWS)
        a[out, :] = part[rows_of(info[8 + i] * ROWS), :]
        b[out, :] = part[rows_of(info[12 + i] * ROWS), :]


def moe_fwd_kernel(info, *refs):
    hs = refs[:8]
    w, wm, chosen = refs[8:11]
    a, b, h2, gu, z, comb = refs[11:17]
    (part,) = refs[17:]
    for i in range(8):
        h2[rows_of(info[i] * ROWS), :] = hs[i][...]

    @pl.loop(0, 4)
    def _(step):
        at = rows_of(step * 256, 256)
        h = h2[at, :]
        logits = dot(h, w[:, QKV + HW : WA])
        lane = lax.broadcasted_iota(jnp.int32, logits.shape, 1)
        live = (lane >= 2) & (lane < 5)
        logits = jnp.where(live, logits, masked_score)
        e = jnp.exp(logits - jnp.max(logits, axis=1, keepdims=True))
        gates = e / jnp.sum(e, axis=1, keepdims=True)
        cb = gates * chosen[at, :].astype(F32)
        comb[at, :] = cb
        full = dot(h, wm[:, :GU])
        gu[at, :] = full
        for x in range(4):
            gate = full[:, x * 256 : x * 256 + 128]
            up = full[:, x * 256 + 128 : x * 256 + 256]
            act = gate * jax.nn.sigmoid(gate) * up
            if x:
                act = act * cb[:, x + 1 : x + 2]
            z[at, x * 128 : (x + 1) * 128] = act.astype(BF16)
        part[at, :] = dot_nt(z[at, :], wm[:, GU:]).astype(BF16)

    for i in range(4):
        out = slice(i * ROWS, (i + 1) * ROWS)
        a[out, :] = part[rows_of(info[8 + i] * ROWS), :]
        b[out, :] = part[rows_of(info[12 + i] * ROWS), :]


def moe_bwd_kernel(info, *refs):
    ds = refs[:8]
    wm, gu, comb = refs[8:11]
    a, b, dm, dgu = refs[11:15]
    (part,) = refs[15:]
    for i in range(8):
        dm[rows_of(info[i] * ROWS), :] = ds[i][...]

    @pl.loop(0, 4)
    def _(step):
        at = rows_of(step * 256, 256)
        dz = dot(dm[at, :], wm[:, GU:])
        cb = comb[at, :]
        lane = lax.broadcasted_iota(jnp.int32, (256, 128), 1)
        extra = jnp.zeros((256, 128), F32)
        for x in range(4):
            gate = gu[at, x * 256 : x * 256 + 128]
            up = gu[at, x * 256 + 128 : x * 256 + 256]
            sig = jax.nn.sigmoid(gate)
            silu = gate * sig
            dact = dz[:, x * 128 : (x + 1) * 128]
            if x:
                dc = jnp.sum(dact * (silu * up), axis=1, keepdims=True)
                high = dc.astype(BF16).astype(F32)
                extra = jnp.where(lane == x + 1, high, extra)
                extra = jnp.where(lane == x + 4, dc - high, extra)
                dact = dact * cb[:, x + 1 : x + 2]
            dgu[at, x * 256 : x * 256 + 128] = (
                dact * up * sig * (1.0 + gate * (1.0 - sig))
            ).astype(BF16)
            dgu[at, x * 256 + 128 : x * 256 + 256] = (dact * silu).astype(BF16)
        part[at, :D] = dot_nt(dgu[at, :], wm[:, :GU]).astype(BF16)
        part[at, D:] = extra.astype(BF16)

    for i in range(4):
        out = slice(i * ROWS, (i + 1) * ROWS)
        a[out, :] = part[rows_of(info[8 + i] * ROWS), :]
        b[out, :] = part[rows_of(info[12 + i] * ROWS), :]


def attn_bwd_kernel(info, *refs):
    ds = refs[:8]
    w, cos, sin, h1, q, k, v, lse, ext = refs[8:17]
    a, b, da, dqkv, dgain = refs[17:22]
    part, dmix, kt, dk, dv = refs[22:]
    for i in range(8):
        da[rows_of(info[i] * ROWS), :] = ds[i][...]

    @pl.loop(0, 4)
    def _(step):
        at = rows_of(step * 256, 256)
        dmix[at, :] = dot(da[at, :], w[:, QKV : QKV + HW]).astype(BF16)
        for j in range(SLOTS):
            col = slice(j * HD, (j + 1) * HD)
            kt[col, at] = k[at, col].astype(F32).T.astype(BF16)

    prefix = info[16]
    for j in range(SLOTS):
        col = slice(j * HD, (j + 1) * HD)
        dk[...] = jnp.zeros_like(dk)
        dv[...] = jnp.zeros_like(dv)

        @pl.loop(0, 4)
        def _(step, j=j, col=col):
            at = rows_of(step * 256, 256)
            qb = q[at, col]
            s = dot_nt(k[:, col], qb) * SCALE
            key = lax.broadcasted_iota(jnp.int32, (SEQ, 256), 0)
            query = lax.broadcasted_iota(jnp.int32, (SEQ, 256), 1) + step * 256
            s = jnp.where(key < jnp.maximum(query + 1, prefix), s, masked_score)
            p = jnp.exp(s - lse[j : j + 1, at])
            dm = dmix[at, col]
            dv[...] += dot(p.astype(BF16), dm)
            dp = dot_nt(v[:, col], dm)
            delta = jnp.sum(dp * p, axis=0, keepdims=True)
            dsb = (SCALE * p * (dp - delta)).astype(BF16)
            dk[...] += dot(dsb, qb)
            dq = dot(kt[col, :], dsb).T
            c, sn = cos[at, :], sin[at, :]
            dqkv[at, col] = (dq * c - half_turn(dq) * sn).astype(BF16)

        u = dk[...]
        dqkv[:, HW + j * HD : HW + (j + 1) * HD] = (
            u * cos[...] - half_turn(u) * sin[...]
        ).astype(BF16)
        dqkv[:, 2 * HW + j * HD : 2 * HW + (j + 1) * HD] = dv[...].astype(BF16)

    dgain[...] = jnp.zeros_like(dgain)

    @pl.loop(0, 4)
    def _(step):
        at = rows_of(step * 256, 256)
        dh = dot_nt(dqkv[at, :], w[:, :QKV])
        part[at, :] = dh.astype(BF16)
        dgain[0:1, :] += jnp.sum(dh * h1[at, :].astype(F32), axis=0, keepdims=True)

    dgain[0:1, :] = dgain[0:1, :] / ext[0:1, :]
    for i in range(4):
        out = slice(i * ROWS, (i + 1) * ROWS)
        a[out, :] = part[rows_of(info[8 + i] * ROWS), :]
        b[out, :] = part[rows_of(info[12 + i] * ROWS), :]


def call(kernel, info, args, outs, scratch, flops):
    total = sum(int(np.prod(x.shape)) * x.dtype.itemsize for x in args)
    total += sum(int(np.prod(s)) * jnp.dtype(t).itemsize for s, t in outs)
    return pl.pallas_call(
        kernel,
        out_shape=[jax.ShapeDtypeStruct(s, t) for s, t in outs],
        in_specs=[pl.BlockSpec(memory_space=pltpu.SMEM)]
        + [pl.BlockSpec(memory_space=pltpu.VMEM)] * len(args),
        out_specs=[pl.BlockSpec(memory_space=pltpu.VMEM)] * len(outs),
        scratch_shapes=[pltpu.VMEM(s, t) for s, t in scratch],
        compiler_params=pltpu.CompilerParams(vmem_limit_bytes=VMEM_LIMIT),
        cost_estimate=pl.CostEstimate(flops=flops, bytes_accessed=total, transcendentals=0),
    )(info, *args)


def exchange(x):
    return lax.ppermute(x, ("c", "xh"), [(0, 0), (1, 2), (2, 1), (3, 3)])


def along_z(x, k):
    return lax.ppermute(x, "z", [(i, (i + k) % 4) for i in range(4)])


def to_other_core(x):
    return lax.ppermute(x, "c", [(0, 1), (1, 0)])


def gather_group(x):
    own = [x] + [along_z(x, k) for k in (1, 2, 3)]
    return own + [to_other_core(part) for part in own]


def scatter_group(a, b):
    got = to_other_core(b)
    s = [
        (a[i * ROWS : (i + 1) * ROWS].astype(F32) + got[i * ROWS : (i + 1) * ROWS].astype(F32))
        for i in range(4)
    ]
    total = s[0]
    for k in (1, 2, 3):
        total = total + along_z(s[k].astype(BF16), k).astype(F32)
    return total


PLANE = ("y", "xl", "xh")


def rope_tables():
    places = jnp.arange(SEQ, dtype=jnp.int32).astype(F32)
    half = HD // 2
    speeds = rope_base ** (-jnp.arange(half, dtype=F32) / half)
    angles = places[:, None] * speeds[None, :]
    c, s = jnp.cos(angles), jnp.sin(angles)
    return jnp.concatenate([c, c], axis=1), jnp.concatenate([-s, s], axis=1)


def on_device(
    tokens, teacher, prefix, routes, attn_gain, w_qkv, w_out, router_w, ffn_gain, w_gate_up, w_down
):
    core, zz = lax.axis_index("c"), lax.axis_index("z")
    near = [core * 4 + (zz + k) % 4 for k in range(4)]
    far = [(1 - core) * 4 + (zz + k) % 4 for k in range(4)]
    back = [0, 3, 2, 1]
    sequence = lax.axis_index(PLANE)
    info = jnp.stack(
        [near[i] for i in back] + [far[i] for i in back] + near + far + [prefix[sequence]]
    ).astype(jnp.int32)

    lanes = jnp.arange(EXT, dtype=jnp.int32)[None, :]
    chosen = (routes[:, 0:1] + 2 == lanes) | (routes[:, 1:2] + 2 == lanes)
    x_all = exchange(jnp.concatenate([tokens, chosen.astype(BF16)], axis=1))
    small = jnp.concatenate([attn_gain[:, None], ffn_gain[:, None], router_w], axis=1)
    raw = exchange(
        jnp.concatenate([w_qkv, w_out, jnp.pad(small, ((0, 0), (0, EXT - 5)))], axis=1)
    )
    n = raw.shape[0]
    heads = raw[:, : 4 * D].reshape(n, 4, GROUPS, HW).transpose(2, 0, 1, 3)
    heads = heads.reshape(GROUPS, n, 4 * HW)
    heads = jnp.pad(heads, ((0, 8 - GROUPS), (0, 0), (0, 0)))
    packed = jnp.concatenate(
        [heads, jnp.broadcast_to(raw[None, :, 4 * D :], (8, n, EXT))], axis=2
    )
    packed = lax.all_to_all(packed, ("c", "z"), split_axis=0, concat_axis=0)
    w = lax.all_gather(packed.reshape(8 * n, WA), PLANE, axis=0, tiled=True)
    lane_pad = 128 - UNITS
    wm_own = jnp.concatenate(
        [
            jnp.pad(w_gate_up, ((0, 0), (0, 0), (0, 0), (0, lane_pad))).reshape(-1, GU),
            jnp.pad(w_down, ((0, 0), (0, 0), (0, lane_pad))).reshape(-1, DN),
        ],
        axis=1,
    )
    wm = lax.all_gather(exchange(wm_own), PLANE, axis=0, tiled=True)
    teach = exchange(teacher)
    cos, sin = rope_tables()

    (a, b, h1, q, k, v, mixed, lse, ext, chosen_all) = call(
        attn_fwd_kernel,
        info,
        gather_group(x_all) + [w, cos, sin],
        [
            ((512, D), BF16),
            ((512, D), BF16),
            ((SEQ, D), BF16),
            ((SEQ, HW), BF16),
            ((SEQ, HW), BF16),
            ((SEQ, HW), BF16),
            ((SEQ, HW), BF16),
            ((8, SEQ), F32),
            ((EXT, D), F32),
            ((SEQ, EXT), BF16),
        ],
        [((SEQ, D), BF16), ((HW, SEQ), BF16)],
        4_000_000_000,
    )
    x = x_all[:, :D].astype(F32)
    x1 = x + scatter_group(a, b)
    r2 = lax.rsqrt(jnp.mean(x1 * x1, axis=1, keepdims=True) + norm_eps)
    n2 = x1 * r2
    gain_two = ext[1:2, :]
    h2 = (n2 * gain_two).astype(BF16)

    a, b, h2_all, gu, z, comb = call(
        moe_fwd_kernel,
        info,
        gather_group(h2) + [w, wm, chosen_all],
        [
            ((512, D), BF16),
            ((512, D), BF16),
            ((SEQ, D), BF16),
            ((SEQ, GU), F32),
            ((SEQ, DN), BF16),
            ((SEQ, EXT), F32),
        ],
        [((SEQ, D), BF16)],
        4_000_000_000,
    )
    y = x1 + scatter_group(a, b)
    diff = y - teach.astype(F32)
    squares = jnp.sum(diff * diff)
    dm = diff.astype(BF16)
    a, b, dm_all, dgu = call(
        moe_bwd_kernel,
        info,
        gather_group(dm) + [wm, gu, comb],
        [((512, D + EXT), BF16), ((512, D + EXT), BF16), ((SEQ, D), BF16), ((SEQ, GU), BF16)],
        [((SEQ, D + EXT), BF16)],
        4_000_000_000,
    )
    dwm = jnp.concatenate(
        [
            lax.dot_general(h2_all, dgu, TN, preferred_element_type=F32).astype(BF16),
            lax.dot_general(dm_all, z, TN, preferred_element_type=F32).astype(BF16),
        ],
        axis=1,
    )
    dwm_own = exchange(lax.psum_scatter(dwm, PLANE, scatter_dimension=0, tiled=True))
    dh2 = scatter_group(a, b)
    dcomb = dh2[:, D + 2 : D + 5] + dh2[:, D + 5 : D + 8]
    router = ext[2:5, :].astype(BF16)
    logits = lax.dot_general(h2, router, NT, preferred_element_type=F32)
    gates = jax.nn.softmax(logits, axis=1)
    dpick = dcomb * x_all[:, D + 2 : D + 5].astype(F32)
    dlogits = (gates * (dpick - jnp.sum(dpick * gates, axis=1, keepdims=True))).astype(BF16)
    d_router = lax.dot_general(dlogits, h2, TN, preferred_element_type=F32)
    dh2 = dh2[:, :D] + jnp.dot(dlogits, router, preferred_element_type=F32)
    d_ffn_gain = jnp.sum(dh2 * n2, axis=0, keepdims=True)
    g2 = dh2 * gain_two
    dx1 = diff + r2 * (g2 - n2 * jnp.mean(g2 * n2, axis=1, keepdims=True))
    da = dx1.astype(BF16)

    a, b, da_all, dqkv, dgain = call(
        attn_bwd_kernel,
        info,
        gather_group(da) + [w, cos, sin, h1, q, k, v, lse, ext],
        [
            ((512, D), BF16),
            ((512, D), BF16),
            ((SEQ, D), BF16),
            ((SEQ, QKV), BF16),
            ((8, D), F32),
        ],
        [
            ((SEQ, D), BF16),
            ((SEQ, HW), BF16),
            ((HW, SEQ), BF16),
            ((SEQ, HD), F32),
            ((SEQ, HD), F32),
        ],
        6_000_000_000,
    )
    sums = jnp.concatenate(
        [dgain[0:1], d_ffn_gain, d_router, jnp.full((1, D), squares / (SEQ * 16), F32)], axis=0
    )
    sums = jnp.pad(sums, ((0, EXT - 6), (0, 0))).T
    dw = jnp.concatenate(
        [
            lax.dot_general(h1, dqkv, TN, preferred_element_type=F32).astype(BF16),
            lax.dot_general(da_all, mixed, TN, preferred_element_type=F32).astype(BF16),
            sums.astype(BF16),
        ],
        axis=1,
    )
    dw = lax.psum_scatter(dw, PLANE, scatter_dimension=0, tiled=True)
    dw = lax.all_to_all(dw.reshape(8, n, WA), ("c", "z"), split_axis=0, concat_axis=0)
    dw_heads = dw[:GROUPS, :, : 4 * HW].reshape(GROUPS, n, 4, HW).transpose(1, 2, 0, 3)
    dw_small = jnp.sum(dw[:, :, 4 * HW :].astype(F32), axis=0)
    d_raw = exchange(
        jnp.concatenate([dw_heads.reshape(n, 4 * D), dw_small.astype(BF16)], axis=1)
    ).astype(F32)

    dh1 = scatter_group(a, b)
    r1 = lax.rsqrt(jnp.mean(x * x, axis=1, keepdims=True) + norm_eps)
    n1 = x * r1
    g1 = dh1 * ext[0:1, :]
    d_tokens = dx1 + r1 * (g1 - n1 * jnp.mean(g1 * n1, axis=1, keepdims=True))

    d_gu = dwm_own[:, :GU].reshape(-1, 4, 2, 128)[..., :UNITS].astype(F32)
    d_dn = dwm_own[:, GU:].reshape(-1, 4, 128)[..., :UNITS].astype(F32)
    return (
        exchange(y.astype(BF16)),
        d_raw[0, 4 * D + 5],
        exchange(d_tokens.astype(BF16)).astype(F32),
        d_raw[:, 4 * D],
        d_raw[:, : 3 * D],
        d_raw[:, 3 * D : 4 * D],
        d_raw[:, 4 * D + 2 : 4 * D + 5],
        d_raw[:, 4 * D + 1],
        d_gu,
        d_dn,
    )


def solution(mesh):
    fine = Mesh(mesh.devices.reshape(4, 2, 2, 2, 4), ("y", "xl", "c", "xh", "z"))
    every = ("y", "xl", "c", "xh", "z")
    rows = P(every, None)
    in_specs = (
        rows,
        rows,
        P(),
        rows,
        P(every),
        rows,
        rows,
        rows,
        P(every),
        P(("y", "xl", "c"), None, None, ("xh", "z")),
        P(("y", "xl", "c"), None, ("xh", "z")),
    )
    out_specs = (
        rows,
        P(),
        rows,
        P(every),
        rows,
        rows,
        rows,
        P(every),
        P(("y", "xl", "c"), None, None, ("xh", "z")),
        P(("y", "xl", "c"), None, ("xh", "z")),
    )
    return jax.shard_map(
        on_device, mesh=fine, in_specs=in_specs, out_specs=out_specs, check_vma=False
    )
```

```python
import functools

import jax
import jax.numpy as jnp
import numpy as np
from jax import lax
from jax.experimental import pallas as pl
from jax.experimental.pallas import tpu as pltpu
from jax.sharding import Mesh, PartitionSpec as P

D = 1280
HD = 128
HEADS = 10
SLOTS = 2
GROUPS = 5
HW = SLOTS * HD
QKV = 3 * HW
EXT = 128
WA = QKV + HW + EXT
ROWS = 128
SEQ = 1024
UNITS = 112
GU = 4 * 2 * 128
DN = 4 * 128
WM = GU + DN
PART = 80
SPLIT_A = 640
SPLIT_M = 768
norm_eps = 1e-06
masked_score = -1e30
rope_base = 10000.0
SCALE = HD ** (-0.5)
F32 = jnp.float32
BF16 = jnp.bfloat16
VMEM_LIMIT = 58 * 1024 * 1024

NT = (((1,), (1,)), ((), ()))
TN = (((0,), (0,)), ((), ()))


def dot(a, b):
    return jnp.dot(a, b, preferred_element_type=F32)


def dot_nt(a, b):
    return lax.dot_general(a, b, NT, preferred_element_type=F32)


def dot_tn(a, b):
    return lax.dot_general(a, b, TN, preferred_element_type=F32)


def rows_of(start, count=ROWS):
    return pl.ds(pl.multiple_of(start, ROWS), count)


def half_turn(u):
    return pltpu.roll(u, HD // 2, 1)


def place_blocks(info, blocks, out, split):
    for j in range(4):
        for m in range(4):
            at = pl.ds(pl.multiple_of(info[32 + j * 4 + m], 16), PART)
            out[at, :split] = blocks[j][m * PART : (m + 1) * PART, :]
            out[at, split:] = blocks[4 + m][j * PART : (j + 1) * PART, :]


def pick_blocks(info, rows, outs, split):
    for j in range(4):
        for m in range(4):
            at = pl.ds(pl.multiple_of(info[48 + j * 4 + m], 16), PART)
            outs[j][m * PART : (m + 1) * PART, :] = rows[at, :split]
            outs[4 + m][j * PART : (j + 1) * PART, :] = rows[at, split:]


def attn_fwd_kernel(info, *refs):
    xs = refs[:8]
    ws = refs[8:16]
    cos, sin = refs[16:18]
    a, b, w, h1, q, k, v, mixed, lse, ext, chosen = refs[18:29]
    part, vt, wp = refs[29:]
    place_blocks(info, ws, wp, SPLIT_A)

    @pl.loop(0, 8)
    def _(p):
        base = pl.multiple_of(p * 2 * PART, 32)
        low = wp[pl.ds(base, PART), :].astype(F32)
        high = wp[pl.ds(base + PART, PART), :].astype(F32)
        half = PART // 2
        for i in range(2):
            cut = slice(i * half, (i + 1) * half)
            w[pl.ds(base + i * PART, PART), :] = jnp.concatenate(
                [low[cut], high[cut]], axis=0
            ).astype(BF16)

    ext_t = w[:, QKV + HW : WA].astype(F32).T
    ext[...] = ext_t
    gain = ext_t[0:1, :]
    for i in range(8):
        blk = xs[i][:, :D].astype(F32)
        r = lax.rsqrt(jnp.mean(blk * blk, axis=1, keepdims=True) + norm_eps)
        at = rows_of(info[i] * ROWS)
        h1[at, :] = (blk * r * gain).astype(BF16)
        chosen[at, :] = xs[i][:, D:]

    @pl.loop(0, 4)
    def _(step):
        at = rows_of(step * 256, 256)
        full = dot(h1[at, :], w[:, :QKV])
        c, s = cos[at, :], sin[at, :]
        for j in range(SLOTS):
            col = slice(j * HD, (j + 1) * HD)
            u = full[:, j * HD : (j + 1) * HD]
            q[at, col] = (u * c + half_turn(u) * s).astype(BF16)
            u = full[:, HW + j * HD : HW + (j + 1) * HD]
            k[at, col] = (u * c + half_turn(u) * s).astype(BF16)
            u = full[:, 2 * HW + j * HD : 2 * HW + (j + 1) * HD]
            v[at, col] = u.astype(BF16)
            vt[col, at] = u.T.astype(BF16)

    prefix = info[16]
    lse[...] = jnp.zeros_like(lse)
    for j in range(SLOTS):
        col = slice(j * HD, (j + 1) * HD)

        @pl.loop(0, 4)
        def _(step, j=j, col=col):
            at = rows_of(step * 256, 256)
            s = dot_nt(k[:, col], q[at, col]) * SCALE
            key = lax.broadcasted_iota(jnp.int32, (SEQ, 256), 0)
            query = lax.broadcasted_iota(jnp.int32, (SEQ, 256), 1) + step * 256
            s = jnp.where(key < jnp.maximum(query + 1, prefix), s, masked_score)
            top = jnp.max(s, axis=0, keepdims=True)
            e = jnp.exp(s - top)
            total = jnp.sum(e, axis=0, keepdims=True)
            pn = (e * (1.0 / total)).astype(BF16)
            mixed[at, col] = dot(vt[col, :], pn).T.astype(BF16)
            lse[j : j + 1, at] = top + jnp.log(total)

    @pl.loop(0, 4)
    def _(step):
        at = rows_of(step * 256, 256)
        part[at, :] = dot_nt(mixed[at, :], w[:, QKV : QKV + HW]).astype(BF16)

    for i in range(4):
        out = slice(i * ROWS, (i + 1) * ROWS)
        a[out, :] = part[rows_of(info[8 + i] * ROWS), :]
        b[out, :] = part[rows_of(info[12 + i] * ROWS), :]


def moe_fwd_kernel(info, *refs):
    hs = refs[:8]
    ws = refs[8:16]
    w, chosen = refs[16:18]
    a, b, wm, h2, gu, z, comb = refs[18:25]
    (part,) = refs[25:]
    place_blocks(info, ws, wm, SPLIT_M)
    for i in range(8):
        h2[rows_of(info[i] * ROWS), :] = hs[i][...]

    @pl.loop(0, 4)
    def _(step):
        at = rows_of(step * 256, 256)
        h = h2[at, :]
        logits = dot(h, w[:, QKV + HW : WA])
        lane = lax.broadcasted_iota(jnp.int32, logits.shape, 1)
        live = (lane >= 2) & (lane < 5)
        logits = jnp.where(live, logits, masked_score)
        e = jnp.exp(logits - jnp.max(logits, axis=1, keepdims=True))
        gates = e / jnp.sum(e, axis=1, keepdims=True)
        cb = gates * chosen[at, :].astype(F32)
        comb[at, :] = cb
        full = dot(h, wm[:, :GU])
        gu[at, :] = full
        for x in range(4):
            gate = full[:, x * 256 : x * 256 + 128]
            up = full[:, x * 256 + 128 : x * 256 + 256]
            act = gate * jax.nn.sigmoid(gate) * up
            if x:
                act = act * cb[:, x + 1 : x + 2]
            z[at, x * 128 : (x + 1) * 128] = act.astype(BF16)
        part[at, :] = dot_nt(z[at, :], wm[:, GU:]).astype(BF16)

    for i in range(4):
        out = slice(i * ROWS, (i + 1) * ROWS)
        a[out, :] = part[rows_of(info[8 + i] * ROWS), :]
        b[out, :] = part[rows_of(info[12 + i] * ROWS), :]


def moe_bwd_kernel(info, *refs):
    ds = refs[:8]
    wm, gu, comb = refs[8:11]
    a, b, dm, dgu = refs[11:15]
    (part,) = refs[15:]
    for i in range(8):
        dm[rows_of(info[i] * ROWS), :] = ds[i][...]

    @pl.loop(0, 4)
    def _(step):
        at = rows_of(step * 256, 256)
        dz = dot(dm[at, :], wm[:, GU:])
        cb = comb[at, :]
        lane = lax.broadcasted_iota(jnp.int32, (256, 128), 1)
        extra = jnp.zeros((256, 128), F32)
        for x in range(4):
            gate = gu[at, x * 256 : x * 256 + 128]
            up = gu[at, x * 256 + 128 : x * 256 + 256]
            sig = jax.nn.sigmoid(gate)
            silu = gate * sig
            dact = dz[:, x * 128 : (x + 1) * 128]
            if x:
                dc = jnp.sum(dact * (silu * up), axis=1, keepdims=True)
                high = dc.astype(BF16).astype(F32)
                extra = jnp.where(lane == x + 1, high, extra)
                extra = jnp.where(lane == x + 4, dc - high, extra)
                dact = dact * cb[:, x + 1 : x + 2]
            dgu[at, x * 256 : x * 256 + 128] = (
                dact * up * sig * (1.0 + gate * (1.0 - sig))
            ).astype(BF16)
            dgu[at, x * 256 + 128 : x * 256 + 256] = (dact * silu).astype(BF16)
        part[at, :D] = dot_nt(dgu[at, :], wm[:, :GU]).astype(BF16)
        part[at, D:] = extra.astype(BF16)

    for i in range(4):
        out = slice(i * ROWS, (i + 1) * ROWS)
        a[out, :] = part[rows_of(info[8 + i] * ROWS), :]
        b[out, :] = part[rows_of(info[12 + i] * ROWS), :]


def moe_grad_kernel(info, *refs):
    h2, dgu, dm, z = refs[:4]
    outs = refs[4:12]
    (rows,) = refs[12:]
    for i in range(2):
        cut = slice(i * 640, (i + 1) * 640)
        rows[cut, :GU] = dot_tn(h2[:, cut], dgu[...]).astype(BF16)
        rows[cut, GU:] = dot_tn(dm[:, cut], z[...]).astype(BF16)
    pick_blocks(info, rows, outs, SPLIT_M)


def attn_bwd_kernel(info, *refs):
    ds = refs[:8]
    w, cos, sin, h1, q, k, v, mixed, lse, sums = refs[8:18]
    outs = refs[18:26]
    dqkv = refs[26]
    da, dmix, kt, dk, dv, rows = refs[27:]
    for i in range(8):
        da[rows_of(info[i] * ROWS), :] = ds[i][...]

    @pl.loop(0, 4)
    def _(step):
        at = rows_of(step * 256, 256)
        dmix[at, :] = dot(da[at, :], w[:, QKV : QKV + HW]).astype(BF16)
        for j in range(SLOTS):
            col = slice(j * HD, (j + 1) * HD)
            kt[col, at] = k[at, col].astype(F32).T.astype(BF16)

    prefix = info[16]
    for j in range(SLOTS):
        col = slice(j * HD, (j + 1) * HD)
        dk[...] = jnp.zeros_like(dk)
        dv[...] = jnp.zeros_like(dv)

        @pl.loop(0, 4)
        def _(step, j=j, col=col):
            at = rows_of(step * 256, 256)
            qb = q[at, col]
            s = dot_nt(k[:, col], qb) * SCALE
            key = lax.broadcasted_iota(jnp.int32, (SEQ, 256), 0)
            query = lax.broadcasted_iota(jnp.int32, (SEQ, 256), 1) + step * 256
            s = jnp.where(key < jnp.maximum(query + 1, prefix), s, masked_score)
            p = jnp.exp(s - lse[j : j + 1, at])
            dm = dmix[at, col]
            dv[...] += dot(p.astype(BF16), dm)
            dp = dot_nt(v[:, col], dm)
            delta = jnp.sum(dp * p, axis=0, keepdims=True)
            dsb = (SCALE * p * (dp - delta)).astype(BF16)
            dk[...] += dot(dsb, qb)
            dq = dot(kt[col, :], dsb).T
            c, sn = cos[at, :], sin[at, :]
            dqkv[at, col] = (dq * c - half_turn(dq) * sn).astype(BF16)

        u = dk[...]
        dqkv[:, HW + j * HD : HW + (j + 1) * HD] = (
            u * cos[...] - half_turn(u) * sin[...]
        ).astype(BF16)
        dqkv[:, 2 * HW + j * HD : 2 * HW + (j + 1) * HD] = dv[...].astype(BF16)

    half = PART // 2
    for i in range(2):
        cut = slice(i * 640, (i + 1) * 640)
        dw = dot_tn(h1[:, cut], dqkv[...])
        do = dot_tn(da[:, cut], mixed[...])
        tail = w[cut, QKV + HW : WA].astype(F32)
        gain = jnp.sum(dw * w[cut, :QKV].astype(F32), axis=1, keepdims=True) / tail[:, 0:1]
        extra = sums[:, cut].T
        lane = lax.broadcasted_iota(jnp.int32, extra.shape, 1)
        extra = jnp.where(lane == 0, gain, extra)
        full = jnp.concatenate([dw, do, extra], axis=1)
        for p in range(4):
            for g in range(2):
                top = p * 2 * PART + g * half
                to = i * 640 + (p * 2 + g) * PART
                rows[to : to + PART, :] = jnp.concatenate(
                    [full[top : top + half], full[top + PART : top + PART + half]], axis=0
                ).astype(BF16)
    pick_blocks(info, rows, outs, SPLIT_A)


def attn_in_kernel(info, *refs):
    w, dqkv = refs[:2]
    a, b = refs[2:4]
    (part,) = refs[4:]

    @pl.loop(0, 4)
    def _(step):
        at = rows_of(step * 256, 256)
        part[at, :] = dot_nt(dqkv[at, :], w[:, :QKV]).astype(BF16)

    for i in range(4):
        out = slice(i * ROWS, (i + 1) * ROWS)
        a[out, :] = part[rows_of(info[8 + i] * ROWS), :]
        b[out, :] = part[rows_of(info[12 + i] * ROWS), :]


def call(kernel, info, args, outs, scratch, flops):
    total = sum(int(np.prod(x.shape)) * x.dtype.itemsize for x in args)
    total += sum(int(np.prod(s)) * jnp.dtype(t).itemsize for s, t in outs)
    return pl.pallas_call(
        kernel,
        out_shape=[jax.ShapeDtypeStruct(s, t) for s, t in outs],
        in_specs=[pl.BlockSpec(memory_space=pltpu.SMEM)]
        + [pl.BlockSpec(memory_space=pltpu.VMEM)] * len(args),
        out_specs=[pl.BlockSpec(memory_space=pltpu.VMEM)] * len(outs),
        scratch_shapes=[pltpu.VMEM(s, t) for s, t in scratch],
        compiler_params=pltpu.CompilerParams(vmem_limit_bytes=VMEM_LIMIT),
        cost_estimate=pl.CostEstimate(flops=flops, bytes_accessed=total, transcendentals=0),
    )(info, *args)


def exchange(x):
    return lax.ppermute(x, ("c", "xh"), [(0, 0), (1, 2), (2, 1), (3, 3)])


def along_z(x, k):
    return lax.ppermute(x, "z", [(i, (i + k) % 4) for i in range(4)])


def along_y(x, k):
    return lax.ppermute(x, "y", [(i, (i + k) % 4) for i in range(4)])


def along_x(x, k):
    place = [0, 2, 1, 3]
    return lax.ppermute(x, ("xl", "xh"), [(place[i], place[(i + k) % 4]) for i in range(4)])


def gather_plane(x, split):
    a, b = x[:, :split], x[:, split:]
    a = jnp.concatenate([a] + [along_x(a, k) for k in (1, 2, 3)], axis=0)
    b = jnp.concatenate([b] + [along_y(b, k) for k in (1, 2, 3)], axis=0)
    return [a] + [along_y(a, k) for k in (1, 2, 3)] + [b] + [along_x(b, k) for k in (1, 2, 3)]


def add_parts(parts, move):
    total = parts[0].astype(F32)
    for k in (1, 2, 3):
        total = total + move(parts[k], k).astype(F32)
    return total.astype(BF16)


def scatter_plane(blocks):
    a = add_parts(blocks[:4], along_y)
    b = add_parts(blocks[4:], along_x)
    a = add_parts([a[i * PART : (i + 1) * PART] for i in range(4)], along_x)
    b = add_parts([b[i * PART : (i + 1) * PART] for i in range(4)], along_y)
    return jnp.concatenate([a, b], axis=1)


def to_other_core(x):
    return lax.ppermute(x, "c", [(0, 1), (1, 0)])


def gather_group(x):
    own = [x] + [along_z(x, k) for k in (1, 2, 3)]
    return own + [to_other_core(part) for part in own]


def scatter_group(a, b):
    got = to_other_core(b)
    s = [
        (a[i * ROWS : (i + 1) * ROWS].astype(F32) + got[i * ROWS : (i + 1) * ROWS].astype(F32))
        for i in range(4)
    ]
    total = s[0]
    for k in (1, 2, 3):
        total = total + along_z(s[k].astype(BF16), k).astype(F32)
    return total


PLANE = ("y", "xl", "xh")


def rope_tables():
    places = jnp.arange(SEQ, dtype=jnp.int32).astype(F32)
    half = HD // 2
    speeds = rope_base ** (-jnp.arange(half, dtype=F32) / half)
    angles = places[:, None] * speeds[None, :]
    c, s = jnp.cos(angles), jnp.sin(angles)
    return jnp.concatenate([c, c], axis=1), jnp.concatenate([-s, s], axis=1)


def on_device(
    tokens, teacher, prefix, routes, attn_gain, w_qkv, w_out, router_w, ffn_gain, w_gate_up, w_down
):
    core, zz = lax.axis_index("c"), lax.axis_index("z")
    near = [core * 4 + (zz + k) % 4 for k in range(4)]
    far = [(1 - core) * 4 + (zz + k) % 4 for k in range(4)]
    back = [0, 3, 2, 1]
    sequence = lax.axis_index(PLANE)
    yy = lax.axis_index("y")
    xx = lax.axis_index("xh") * 2 + lax.axis_index("xl")

    def place(dy, dx):
        y, x = (yy + dy) % 4, (xx + dx) % 4
        return (y * 4 + x % 2 * 2 + x // 2) * PART

    info = jnp.stack(
        [near[i] for i in back]
        + [far[i] for i in back]
        + near
        + far
        + [prefix[sequence]]
        + [jnp.int32(0)] * 15
        + [place(-j, -m) for j in range(4) for m in range(4)]
        + [place(j, m) for j in range(4) for m in range(4)]
    ).astype(jnp.int32)

    lanes = jnp.arange(EXT, dtype=jnp.int32)[None, :]
    chosen = (routes[:, 0:1] + 2 == lanes) | (routes[:, 1:2] + 2 == lanes)
    x_all = exchange(jnp.concatenate([tokens, chosen.astype(BF16)], axis=1))
    small = jnp.concatenate([attn_gain[:, None], ffn_gain[:, None], router_w], axis=1)
    raw = jnp.concatenate([w_qkv, w_out, jnp.pad(small, ((0, 0), (0, EXT - 5)))], axis=1)
    n = raw.shape[0]
    heads = raw[:, : 4 * D].reshape(n, 4, GROUPS, HW).transpose(2, 0, 1, 3)
    heads = heads.reshape(GROUPS, n, 4 * HW)
    heads = jnp.pad(heads, ((0, 8 - GROUPS), (0, 0), (0, 0)))
    packed = jnp.concatenate(
        [heads, jnp.broadcast_to(raw[None, :, 4 * D :], (8, n, EXT))], axis=2
    )
    packed = lax.all_to_all(packed, ("c", "z"), split_axis=0, concat_axis=0)
    w_blocks = gather_plane(packed.reshape(8 * n, WA), SPLIT_A)
    lane_pad = 128 - UNITS
    wm_own = jnp.concatenate(
        [
            jnp.pad(w_gate_up, ((0, 0), (0, 0), (0, 0), (0, lane_pad))).reshape(-1, GU),
            jnp.pad(w_down, ((0, 0), (0, 0), (0, lane_pad))).reshape(-1, DN),
        ],
        axis=1,
    )
    wm_own, _ = lax.optimization_barrier((exchange(wm_own), w_blocks[3]))
    wm_blocks = gather_plane(wm_own, SPLIT_M)
    teach = exchange(teacher)
    cos, sin = rope_tables()

    (a, b, w, h1, q, k, v, mixed, lse, ext, chosen_all) = call(
        attn_fwd_kernel,
        info,
        gather_group(x_all) + w_blocks + [cos, sin],
        [
            ((512, D), BF16),
            ((512, D), BF16),
            ((D, WA), BF16),
            ((SEQ, D), BF16),
            ((SEQ, HW), BF16),
            ((SEQ, HW), BF16),
            ((SEQ, HW), BF16),
            ((SEQ, HW), BF16),
            ((8, SEQ), F32),
            ((EXT, D), F32),
            ((SEQ, EXT), BF16),
        ],
        [((SEQ, D), BF16), ((HW, SEQ), BF16), ((D, WA), BF16)],
        4_000_000_000,
    )
    x = x_all[:, :D].astype(F32)
    x1 = x + scatter_group(a, b)
    r2 = lax.rsqrt(jnp.mean(x1 * x1, axis=1, keepdims=True) + norm_eps)
    n2 = x1 * r2
    gain_two = ext[1:2, :]
    h2 = (n2 * gain_two).astype(BF16)

    a, b, wm, h2_all, gu, z, comb = call(
        moe_fwd_kernel,
        info,
        gather_group(h2) + wm_blocks + [w, chosen_all],
        [
            ((512, D), BF16),
            ((512, D), BF16),
            ((D, WM), BF16),
            ((SEQ, D), BF16),
            ((SEQ, GU), F32),
            ((SEQ, DN), BF16),
            ((SEQ, EXT), F32),
        ],
        [((SEQ, D), BF16)],
        4_000_000_000,
    )
    y = x1 + scatter_group(a, b)
    diff = y - teach.astype(F32)
    squares = jnp.sum(diff * diff)
    dm = diff.astype(BF16)
    a, b, dm_all, dgu = call(
        moe_bwd_kernel,
        info,
        gather_group(dm) + [wm, gu, comb],
        [((512, D + EXT), BF16), ((512, D + EXT), BF16), ((SEQ, D), BF16), ((SEQ, GU), BF16)],
        [((SEQ, D + EXT), BF16)],
        4_000_000_000,
    )
    dwm_blocks = call(
        moe_grad_kernel,
        info,
        [h2_all, dgu, dm_all, z],
        [((4 * PART, SPLIT_M), BF16)] * 4 + [((4 * PART, WM - SPLIT_M), BF16)] * 4,
        [((D, WM), BF16)],
        4_000_000_000,
    )
    dwm_own = exchange(scatter_plane(dwm_blocks))
    dh2 = scatter_group(a, b)
    dcomb = dh2[:, D + 2 : D + 5] + dh2[:, D + 5 : D + 8]
    router = ext[2:5, :].astype(BF16)
    logits = lax.dot_general(h2, router, NT, preferred_element_type=F32)
    gates = jax.nn.softmax(logits, axis=1)
    dpick = dcomb * x_all[:, D + 2 : D + 5].astype(F32)
    dlogits = (gates * (dpick - jnp.sum(dpick * gates, axis=1, keepdims=True))).astype(BF16)
    d_router = lax.dot_general(dlogits, h2, TN, preferred_element_type=F32)
    dh2 = dh2[:, :D] + jnp.dot(dlogits, router, preferred_element_type=F32)
    d_ffn_gain = jnp.sum(dh2 * n2, axis=0, keepdims=True)
    g2 = dh2 * gain_two
    dx1 = diff + r2 * (g2 - n2 * jnp.mean(g2 * n2, axis=1, keepdims=True))
    da = dx1.astype(BF16)

    sums = jnp.concatenate(
        [
            jnp.zeros((1, D), F32),
            d_ffn_gain,
            d_router,
            jnp.full((1, D), squares / (SEQ * 16), F32),
        ],
        axis=0,
    )
    sums = jnp.pad(sums, ((0, EXT - 6), (0, 0)))
    *dw_blocks, dqkv = call(
        attn_bwd_kernel,
        info,
        gather_group(da) + [w, cos, sin, h1, q, k, v, mixed, lse, sums],
        [((4 * PART, SPLIT_A), BF16)] * 4
        + [((4 * PART, WA - SPLIT_A), BF16)] * 4
        + [((SEQ, QKV), BF16)],
        [
            ((SEQ, D), BF16),
            ((SEQ, HW), BF16),
            ((HW, SEQ), BF16),
            ((SEQ, HD), F32),
            ((SEQ, HD), F32),
            ((D, WA), BF16),
        ],
        6_000_000_000,
    )
    a, b = call(
        attn_in_kernel,
        info,
        [w, dqkv],
        [((512, D), BF16), ((512, D), BF16)],
        [((SEQ, D), BF16)],
        2_000_000_000,
    )
    dw = scatter_plane(dw_blocks)
    dw = lax.all_to_all(dw.reshape(8, n, WA), ("c", "z"), split_axis=0, concat_axis=0)
    dw_heads = dw[:GROUPS, :, : 4 * HW].reshape(GROUPS, n, 4, HW).transpose(1, 2, 0, 3)
    dw_small = jnp.sum(dw[:, :, 4 * HW :].astype(F32), axis=0)
    d_raw = jnp.concatenate(
        [dw_heads.reshape(n, 4 * D).astype(F32), dw_small], axis=1
    )

    dh1 = scatter_group(a, b)
    r1 = lax.rsqrt(jnp.mean(x * x, axis=1, keepdims=True) + norm_eps)
    n1 = x * r1
    g1 = dh1 * ext[0:1, :]
    d_tokens = dx1 + r1 * (g1 - n1 * jnp.mean(g1 * n1, axis=1, keepdims=True))

    d_gu = dwm_own[:, :GU].reshape(-1, 4, 2, 128)[..., :UNITS].astype(F32)
    d_dn = dwm_own[:, GU:].reshape(-1, 4, 128)[..., :UNITS].astype(F32)
    return (
        exchange(y.astype(BF16)),
        d_raw[0, 4 * D + 5],
        exchange(d_tokens.astype(BF16)).astype(F32),
        d_raw[:, 4 * D],
        d_raw[:, : 3 * D],
        d_raw[:, 3 * D : 4 * D],
        d_raw[:, 4 * D + 2 : 4 * D + 5],
        d_raw[:, 4 * D + 1],
        d_gu,
        d_dn,
    )


def solution(mesh):
    fine = Mesh(mesh.devices.reshape(4, 2, 2, 2, 4), ("y", "xl", "c", "xh", "z"))
    every = ("y", "xl", "c", "xh", "z")
    rows = P(every, None)
    in_specs = (
        rows,
        rows,
        P(),
        rows,
        P(every),
        rows,
        rows,
        rows,
        P(every),
        P(("y", "xl", "c"), None, None, ("xh", "z")),
        P(("y", "xl", "c"), None, ("xh", "z")),
    )
    out_specs = (
        rows,
        P(),
        rows,
        P(every),
        rows,
        rows,
        rows,
        P(every),
        P(("y", "xl", "c"), None, None, ("xh", "z")),
        P(("y", "xl", "c"), None, ("xh", "z")),
    )
    return jax.shard_map(
        on_device, mesh=fine, in_specs=in_specs, out_specs=out_specs, check_vma=False
    )
```

```python
import functools

import jax
import jax.numpy as jnp
import numpy as np
from jax import lax
from jax.experimental import pallas as pl
from jax.experimental.pallas import tpu as pltpu
from jax.sharding import Mesh, PartitionSpec as P

D = 1280
HD = 128
HEADS = 10
SLOTS = 2
GROUPS = 5
HW = SLOTS * HD
QKV = 3 * HW
EXT = 128
WQ = QKV + EXT
WA = WQ + HW
ROWS = 128
SEQ = 1024
UNITS = 112
GU = 4 * 2 * 128
DN = 4 * 128
WM = GU + DN
PART = 80
SPLIT_A = 640
SPLIT_M = 768
norm_eps = 1e-06
masked_score = -1e30
rope_base = 10000.0
SCALE = HD ** (-0.5)
F32 = jnp.float32
BF16 = jnp.bfloat16
MIB = 1024 * 1024
LIM = (52, 12, 10, 10, 12, 53, 10)

NT = (((1,), (1,)), ((), ()))
TN = (((0,), (0,)), ((), ()))


def dot(a, b):
    return jnp.dot(a, b, preferred_element_type=F32)


def dot_nt(a, b):
    return lax.dot_general(a, b, NT, preferred_element_type=F32)


def dot_tn(a, b):
    return lax.dot_general(a, b, TN, preferred_element_type=F32)


def rows_of(start, count=ROWS):
    return pl.ds(pl.multiple_of(start, ROWS), count)


def half_turn(u):
    return pltpu.roll(u, HD // 2, 1)


def pick_blocks(info, rows, outs, split):
    for j in range(4):
        for m in range(4):
            at = pl.ds(pl.multiple_of(info[32 + j * 4 + m], 16), PART)
            outs[j][m * PART : (m + 1) * PART, :] = rows[at, :split]
            outs[4 + m][j * PART : (j + 1) * PART, :] = rows[at, split:]


def natural_rows(placed, out, first):
    half = PART // 2
    columns = slice(first, first + out.shape[1])
    for p in range(8):
        at = (p // 2 * 4 + p % 2) * PART
        low = placed[at : at + PART, columns].astype(F32)
        high = placed[at + 2 * PART : at + 3 * PART, columns].astype(F32)
        for i in range(2):
            cut = slice(i * half, (i + 1) * half)
            to = (2 * p + i) * PART
            out[to : to + PART, :] = jnp.concatenate([low[cut], high[cut]], axis=0).astype(BF16)


def place_kernel(info, *refs):
    x, chosen = refs[8:]
    for i in range(8):
        at = rows_of(info[i] * ROWS)
        x[at, :] = refs[i][:, :D]
        chosen[at, :] = refs[i][:, D:]


def attn_fwd_kernel(info, w_far, x, cos, sin, *refs):
    saved = refs[:7]
    a, b, wext, lse, ext = refs[7:12]
    w, h1, q, k, v, mixed, wo, wp, vt, part, sems = refs[12:]
    held = [w, h1, q, k, v, mixed, wo]

    def keep(i):
        return pltpu.make_async_copy(held[i], saved[i], sems.at[i])

    load = pltpu.make_async_copy(w_far, wp, sems.at[7])
    load.start()
    load.wait()
    natural_rows(wp, w, 0)
    natural_rows(wp, wo, WQ)
    keep(0).start()
    keep(6).start()
    wext[...] = w[:, QKV:]
    ext_t = w[:, QKV:].astype(F32).T
    ext[...] = ext_t
    gain = ext_t[0:1, :]

    @pl.loop(0, 4)
    def _(step):
        at = rows_of(step * 256, 256)
        blk = x[at, :].astype(F32)
        r = lax.rsqrt(jnp.mean(blk * blk, axis=1, keepdims=True) + norm_eps)
        h = (blk * r * gain).astype(BF16)
        h1[at, :] = h
        full = dot(h, w[:, :QKV])
        c, s = cos[at, :], sin[at, :]
        for j in range(SLOTS):
            col = slice(j * HD, (j + 1) * HD)
            u = full[:, j * HD : (j + 1) * HD]
            q[at, col] = (u * c + half_turn(u) * s).astype(BF16)
            u = full[:, HW + j * HD : HW + (j + 1) * HD]
            k[at, col] = (u * c + half_turn(u) * s).astype(BF16)
            u = full[:, 2 * HW + j * HD : 2 * HW + (j + 1) * HD]
            v[at, col] = u.astype(BF16)
            vt[col, at] = u.T.astype(BF16)

    for i in range(1, 5):
        keep(i).start()
    prefix = info[16]
    lse[...] = jnp.zeros_like(lse)
    for j in range(SLOTS):
        col = slice(j * HD, (j + 1) * HD)

        @pl.loop(0, 4)
        def _(step, j=j, col=col):
            at = rows_of(step * 256, 256)
            s = dot_nt(k[:, col], q[at, col]) * SCALE
            key = lax.broadcasted_iota(jnp.int32, (SEQ, 256), 0)
            query = lax.broadcasted_iota(jnp.int32, (SEQ, 256), 1) + step * 256
            s = jnp.where(key < jnp.maximum(query + 1, prefix), s, masked_score)
            top = jnp.max(s, axis=0, keepdims=True)
            e = jnp.exp(s - top)
            total = jnp.sum(e, axis=0, keepdims=True)
            pn = (e * (1.0 / total)).astype(BF16)
            mixed[at, col] = dot(vt[col, :], pn).T.astype(BF16)
            lse[j : j + 1, at] = top + jnp.log(total)

    keep(5).start()

    @pl.loop(0, 4)
    def _(step):
        at = rows_of(step * 256, 256)
        part[at, :] = dot_nt(mixed[at, :], wo[...]).astype(BF16)

    give_blocks(info, part, a, b)
    for i in range(7):
        keep(i).wait()


def give_blocks(info, part, a, b):
    for i in range(4):
        out = slice(i * ROWS, (i + 1) * ROWS)
        a[out, :] = part[rows_of(info[8 + i] * ROWS), :]
        b[out, :] = part[rows_of(info[12 + i] * ROWS), :]


def moe_fwd_kernel(info, *refs):
    hs = refs[:8]
    wm, wext, chosen = refs[8:11]
    a, b, h2, gu, z, comb = refs[11:17]
    (part,) = refs[17:]
    for i in range(8):
        h2[rows_of(info[i] * ROWS), :] = hs[i][...]

    @pl.loop(0, 4)
    def _(step):
        at = rows_of(step * 256, 256)
        h = h2[at, :]
        logits = dot(h, wext[...])
        lane = lax.broadcasted_iota(jnp.int32, logits.shape, 1)
        live = (lane >= 2) & (lane < 5)
        logits = jnp.where(live, logits, masked_score)
        e = jnp.exp(logits - jnp.max(logits, axis=1, keepdims=True))
        gates = e / jnp.sum(e, axis=1, keepdims=True)
        cb = gates * chosen[at, :].astype(F32)
        comb[at, :] = cb
        full = dot(h, wm[:, :GU])
        gu[at, :] = full
        for x in range(4):
            gate = full[:, x * 256 : x * 256 + 128]
            up = full[:, x * 256 + 128 : x * 256 + 256]
            act = gate * jax.nn.sigmoid(gate) * up
            if x:
                act = act * cb[:, x + 1 : x + 2]
            z[at, x * 128 : (x + 1) * 128] = act.astype(BF16)
        part[at, :] = dot_nt(z[at, :], wm[:, GU:]).astype(BF16)

    give_blocks(info, part, a, b)


def moe_bwd_kernel(info, *refs):
    ds = refs[:8]
    wm, gu, comb = refs[8:11]
    a, b, dm, dgu = refs[11:15]
    (part,) = refs[15:]
    for i in range(8):
        dm[rows_of(info[i] * ROWS), :] = ds[i][...]

    @pl.loop(0, 4)
    def _(step):
        at = rows_of(step * 256, 256)
        dz = dot(dm[at, :], wm[:, GU:])
        cb = comb[at, :]
        lane = lax.broadcasted_iota(jnp.int32, (256, 128), 1)
        extra = jnp.zeros((256, 128), F32)
        for x in range(4):
            gate = gu[at, x * 256 : x * 256 + 128]
            up = gu[at, x * 256 + 128 : x * 256 + 256]
            sig = jax.nn.sigmoid(gate)
            silu = gate * sig
            dact = dz[:, x * 128 : (x + 1) * 128]
            if x:
                dc = jnp.sum(dact * (silu * up), axis=1, keepdims=True)
                high = dc.astype(BF16).astype(F32)
                extra = jnp.where(lane == x + 1, high, extra)
                extra = jnp.where(lane == x + 4, dc - high, extra)
                dact = dact * cb[:, x + 1 : x + 2]
            dgu[at, x * 256 : x * 256 + 128] = (
                dact * up * sig * (1.0 + gate * (1.0 - sig))
            ).astype(BF16)
            dgu[at, x * 256 + 128 : x * 256 + 256] = (dact * silu).astype(BF16)
        part[at, :D] = dot_nt(dgu[at, :], wm[:, :GU]).astype(BF16)
        part[at, D:] = extra.astype(BF16)

    give_blocks(info, part, a, b)


def moe_grad_kernel(info, *refs):
    h2, dgu, dm, z, saved, rows, sems = refs

    def keep(i):
        cut = slice(i * 640, (i + 1) * 640)
        return pltpu.make_async_copy(rows.at[cut, :], saved.at[cut, :], sems.at[i])

    for i in range(2):
        cut = slice(i * 640, (i + 1) * 640)
        rows[cut, :GU] = dot_tn(h2[:, cut], dgu[...]).astype(BF16)
        rows[cut, GU:] = dot_tn(dm[:, cut], z[...]).astype(BF16)
        keep(i).start()
    for i in range(2):
        keep(i).wait()


def attn_bwd_kernel(info, *refs):
    ds = refs[:8]
    far = refs[8:17]
    lse, sums = refs[17:19]
    outs = refs[19:27]
    dqkv = refs[27]
    near = refs[28:37]
    wo, k, q, v, cos, sin, h1, mixed, w = near
    da, dmix, kt, dk, dv, rows, sems = refs[37:]
    loads = [pltpu.make_async_copy(a, b, sems.at[i]) for i, (a, b) in enumerate(zip(far, near))]
    for load in loads:
        load.start()
    for i in range(8):
        da[rows_of(info[i] * ROWS), :] = ds[i][...]
    loads[0].wait()
    loads[1].wait()

    @pl.loop(0, 4)
    def _(step):
        at = rows_of(step * 256, 256)
        dmix[at, :] = dot(da[at, :], wo[...]).astype(BF16)
        for j in range(SLOTS):
            col = slice(j * HD, (j + 1) * HD)
            kt[col, at] = k[at, col].astype(F32).T.astype(BF16)

    for i in range(2, 6):
        loads[i].wait()
    prefix = info[16]
    for j in range(SLOTS):
        col = slice(j * HD, (j + 1) * HD)
        dk[...] = jnp.zeros_like(dk)
        dv[...] = jnp.zeros_like(dv)

        @pl.loop(0, 4)
        def _(step, j=j, col=col):
            at = rows_of(step * 256, 256)
            qb = q[at, col]
            s = dot_nt(k[:, col], qb) * SCALE
            key = lax.broadcasted_iota(jnp.int32, (SEQ, 256), 0)
            query = lax.broadcasted_iota(jnp.int32, (SEQ, 256), 1) + step * 256
            s = jnp.where(key < jnp.maximum(query + 1, prefix), s, masked_score)
            p = jnp.exp(s - lse[j : j + 1, at])
            dm = dmix[at, col]
            dv[...] += dot(p.astype(BF16), dm)
            dp = dot_nt(v[:, col], dm)
            delta = jnp.sum(dp * p, axis=0, keepdims=True)
            dsb = (SCALE * p * (dp - delta)).astype(BF16)
            dk[...] += dot(dsb, qb)
            dq = dot(kt[col, :], dsb).T
            c, sn = cos[at, :], sin[at, :]
            dqkv[at, col] = (dq * c - half_turn(dq) * sn).astype(BF16)

        u = dk[...]
        dqkv[:, HW + j * HD : HW + (j + 1) * HD] = (
            u * cos[...] - half_turn(u) * sin[...]
        ).astype(BF16)
        dqkv[:, 2 * HW + j * HD : 2 * HW + (j + 1) * HD] = dv[...].astype(BF16)

    for i in range(6, 9):
        loads[i].wait()
    half = PART // 2
    for i in range(2):
        cut = slice(i * 640, (i + 1) * 640)
        dw = dot_tn(h1[:, cut], dqkv[...])
        do = dot_tn(da[:, cut], mixed[...])
        tail = w[cut, QKV:].astype(F32)
        gain = jnp.sum(dw * w[cut, :QKV].astype(F32), axis=1, keepdims=True) / tail[:, 0:1]
        extra = sums[:, cut].T
        lane = lax.broadcasted_iota(jnp.int32, extra.shape, 1)
        extra = jnp.where(lane == 0, gain, extra)
        full = jnp.concatenate([dw, do, extra], axis=1)
        for p in range(4):
            for g in range(2):
                top = p * 2 * PART + g * half
                to = i * 640 + (p * 2 + g) * PART
                rows[to : to + PART, :] = jnp.concatenate(
                    [full[top : top + half], full[top + PART : top + PART + half]], axis=0
                ).astype(BF16)
    pick_blocks(info, rows, outs, SPLIT_A)


def attn_in_kernel(info, *refs):
    w, dqkv = refs[:2]
    a, b = refs[2:4]
    (part,) = refs[4:]

    @pl.loop(0, 4)
    def _(step):
        at = rows_of(step * 256, 256)
        part[at, :] = dot_nt(dqkv[at, :], w[:, :QKV]).astype(BF16)

    give_blocks(info, part, a, b)


def finish_kernel(info, dw, qkv, out, gains, router, loss):
    for g in range(GROUPS):
        for part in range(3):
            to = part * D + g * HW
            qkv[:, to : to + HW] = dw[g, :, part * HW : (part + 1) * HW].astype(F32)
        out[:, g * HW : (g + 1) * HW] = dw[g, :, QKV : QKV + HW].astype(F32)
    total = dw[0, :, QKV + HW :].astype(F32)
    for g in range(1, 8):
        total = total + dw[g, :, QKV + HW :].astype(F32)
    router[...] = total[:, 2:5]
    loss[...] = total[0:1, 5:6]
    gains[...] = total.T[0:8, :]


def call(kernel, info, args, outs, scratch, flops, mib, far_in=(), far_out=(), sems=0):
    total = sum(int(np.prod(x.shape)) * x.dtype.itemsize for x in args)
    total += sum(int(np.prod(s)) * jnp.dtype(t).itemsize for s, t in outs)

    def spec(far):
        return pl.BlockSpec(memory_space=pltpu.HBM if far else pltpu.VMEM)

    return pl.pallas_call(
        kernel,
        out_shape=[jax.ShapeDtypeStruct(s, t) for s, t in outs],
        in_specs=[pl.BlockSpec(memory_space=pltpu.SMEM)]
        + [spec(i in far_in) for i in range(len(args))],
        out_specs=[spec(i in far_out) for i in range(len(outs))],
        scratch_shapes=[pltpu.VMEM(s, t) for s, t in scratch]
        + ([pltpu.SemaphoreType.DMA((sems,))] if sems else []),
        compiler_params=pltpu.CompilerParams(vmem_limit_bytes=mib * MIB),
        cost_estimate=pl.CostEstimate(flops=flops, bytes_accessed=total, transcendentals=0),
    )(info, *args)


def exchange(x):
    return lax.ppermute(x, ("c", "xh"), [(0, 0), (1, 2), (2, 1), (3, 3)])


def turn_out(x):
    pairs = [(i * 4 + j * 2 + k, j * 4 + k * 2 + i) for i in (0, 1) for j in (0, 1) for k in (0, 1)]
    return lax.ppermute(x, ("xl", "c", "xh"), pairs)


def turn_home(x):
    pairs = [(j * 4 + k * 2 + i, i * 4 + j * 2 + k) for i in (0, 1) for j in (0, 1) for k in (0, 1)]
    return lax.ppermute(x, ("xl", "c", "xh"), pairs)


def along_z(x, k):
    return lax.ppermute(x, "z", [(i, (i + k) % 4) for i in range(4)])


def along_y(x, k):
    return lax.ppermute(x, "y", [(i, (i + k) % 4) for i in range(4)])


def along_x(x, k):
    place = [0, 2, 1, 3]
    return lax.ppermute(x, ("xl", "xh"), [(place[i], place[(i + k) % 4]) for i in range(4)])


def after(x, *deps):
    return lax.optimization_barrier((x, deps))[0]


def add_parts(parts, move):
    total = parts[0].astype(F32)
    for k in (1, 2, 3):
        total = total + move(parts[k], k).astype(F32)
    return total.astype(BF16)


def to_other_core(x):
    return lax.ppermute(x, "c", [(0, 1), (1, 0)])


def gather_group(x, *deps):
    own = [x] + [along_z(x, k) for k in (1, 2, 3)]
    last = after(own[3], *deps) if deps else own[3]
    return own + [to_other_core(part) for part in own[:3] + [last]]


def scatter_group(a, b):
    got = to_other_core(b)
    s = [
        (a[i * ROWS : (i + 1) * ROWS].astype(F32) + got[i * ROWS : (i + 1) * ROWS].astype(F32))
        for i in range(4)
    ]
    total = s[0]
    for k in (1, 2, 3):
        total = total + along_z(s[k].astype(BF16), k).astype(F32)
    return total


def sum_cores(a, b):
    got = to_other_core(b)
    cuts = [slice(k * ROWS, (k + 1) * ROWS) for k in range(4)]
    return [(a[cut].astype(F32) + got[cut].astype(F32)).astype(BF16) for cut in cuts]


def scatter_home(parts):
    total = 0.0
    for k in range(4):
        pairs = [
            (c * 8 + x * 4 + z, x * 8 + c * 4 + (z + k) % 4)
            for c in range(2)
            for x in range(2)
            for z in range(4)
        ]
        total = total + lax.ppermute(parts[k], ("c", "xh", "z"), pairs).astype(F32)
    return total


PLANE = ("y", "xl", "xh")
RING = ("y", "xh", "xl")


def rope_tables():
    places = jnp.arange(SEQ, dtype=jnp.int32).astype(F32)
    half = HD // 2
    speeds = rope_base ** (-jnp.arange(half, dtype=F32) / half)
    angles = places[:, None] * speeds[None, :]
    c, s = jnp.cos(angles), jnp.sin(angles)
    return jnp.concatenate([c, c], axis=1), jnp.concatenate([-s, s], axis=1)


def on_device(
    tokens, teacher, prefix, routes, attn_gain, w_qkv, w_out, router_w, ffn_gain, w_gate_up, w_down
):
    core, zz = lax.axis_index("c"), lax.axis_index("z")
    near = [core * 4 + (zz + k) % 4 for k in range(4)]
    far = [(1 - core) * 4 + (zz + k) % 4 for k in range(4)]
    back = [0, 3, 2, 1]
    sequence = lax.axis_index(PLANE)
    yy = lax.axis_index("y")
    xx = lax.axis_index("xh") * 2 + lax.axis_index("xl")

    def place(dy, dx):
        y, x = (yy + dy) % 4, (xx + dx) % 4
        return (y * 4 + x % 2 * 2 + x // 2) * PART

    info = jnp.stack(
        [near[i] for i in back]
        + [far[i] for i in back]
        + near
        + far
        + [prefix[sequence]]
        + [jnp.int32(0)] * 15
        + [place(j, m) for j in range(4) for m in range(4)]
    ).astype(jnp.int32)

    lanes = jnp.arange(EXT, dtype=jnp.int32)[None, :]
    chosen = (routes[:, 0:1] + 2 == lanes) | (routes[:, 1:2] + 2 == lanes)
    x_all = exchange(jnp.concatenate([tokens, chosen.astype(BF16)], axis=1))
    small = jnp.concatenate([attn_gain[:, None], ffn_gain[:, None], router_w], axis=1)
    raw = jnp.concatenate([w_qkv, w_out, jnp.pad(small, ((0, 0), (0, EXT - 5)))], axis=1)
    n = raw.shape[0]
    heads = raw[:, : 4 * D].reshape(n, 4, GROUPS, HW).transpose(2, 0, 1, 3)
    heads = jnp.pad(heads.reshape(GROUPS, n, 4 * HW), ((0, 8 - GROUPS), (0, 0), (0, 0)))
    extra = jnp.broadcast_to(raw[None, :, 4 * D :], (8, n, EXT))
    packed = jnp.concatenate([heads[:, :, :QKV], extra, heads[:, :, QKV:]], axis=2)
    packed = lax.all_to_all(packed, ("c", "z"), split_axis=0, concat_axis=0).reshape(8 * n, WA)
    lane_pad = 128 - UNITS
    wm_own = jnp.concatenate(
        [
            jnp.pad(w_gate_up, ((0, 0), (0, 0), (0, 0), (0, lane_pad))).reshape(-1, GU),
            jnp.pad(w_down, ((0, 0), (0, 0), (0, lane_pad))).reshape(-1, DN),
        ],
        axis=1,
    )
    wm_own = turn_out(wm_own)
    w_all = lax.all_gather(packed, RING, axis=0, tiled=True)
    x_seq, chosen_all = call(
        place_kernel,
        info,
        gather_group(x_all),
        [((SEQ, D), BF16), ((SEQ, EXT), BF16)],
        [],
        0,
        6,
    )
    wm = lax.all_gather(after(wm_own, w_all, x_seq), RING, axis=0, tiled=True)
    teach = exchange(teacher)
    cos, sin = rope_tables()

    head = ((SEQ, HW), BF16)
    w, h1, q, k, v, mixed, wo, a, b, wext, lse, ext = call(
        attn_fwd_kernel,
        info,
        [w_all, x_seq, cos, sin],
        [
            ((D, WQ), BF16),
            ((SEQ, D), BF16),
            head,
            head,
            head,
            head,
            ((D, HW), BF16),
            ((512, D), BF16),
            ((512, D), BF16),
            ((D, EXT), BF16),
            ((8, SEQ), F32),
            ((EXT, D), F32),
        ],
        [
            ((D, WQ), BF16),
            ((SEQ, D), BF16),
            head,
            head,
            head,
            head,
            ((D, HW), BF16),
            ((D, WA), BF16),
            ((HW, SEQ), BF16),
            ((SEQ, D), BF16),
        ],
        5_000_000_000,
        LIM[0],
        far_in=(0,),
        far_out=range(7),
        sems=8,
    )
    x = x_all[:, :D].astype(F32)
    x1 = x + scatter_group(a, b)
    r2 = lax.rsqrt(jnp.mean(x1 * x1, axis=1, keepdims=True) + norm_eps)
    n2 = x1 * r2
    gain_two = ext[1:2, :]
    h2 = (n2 * gain_two).astype(BF16)

    a, b, h2_all, gu, z, comb = call(
        moe_fwd_kernel,
        info,
        gather_group(h2, wm) + [wm, wext, chosen_all],
        [
            ((512, D), BF16),
            ((512, D), BF16),
            ((SEQ, D), BF16),
            ((SEQ, GU), F32),
            ((SEQ, DN), BF16),
            ((SEQ, EXT), F32),
        ],
        [((SEQ, D), BF16)],
        4_000_000_000,
        LIM[2],
    )
    y = x1 + scatter_group(a, b)
    diff = y - teach.astype(F32)
    squares = jnp.sum(diff * diff)
    dm = diff.astype(BF16)
    a, b, dm_all, dgu = call(
        moe_bwd_kernel,
        info,
        gather_group(dm) + [wm, gu, comb],
        [((512, D + EXT), BF16), ((512, D + EXT), BF16), ((SEQ, D), BF16), ((SEQ, GU), BF16)],
        [((SEQ, D + EXT), BF16)],
        4_000_000_000,
        LIM[3],
    )
    (dwm,) = call(
        moe_grad_kernel,
        info,
        [h2_all, dgu, dm_all, z],
        [((D, WM), BF16)],
        [((D, WM), BF16)],
        4_000_000_000,
        LIM[4],
        far_out=(0,),
        sems=2,
    )
    dwm_own = lax.psum_scatter(dwm, RING, scatter_dimension=0, tiled=True)
    dh2 = scatter_group(a, b)
    dcomb = dh2[:, D + 2 : D + 5] + dh2[:, D + 5 : D + 8]
    router = ext[2:5, :].astype(BF16)
    logits = lax.dot_general(h2, router, NT, preferred_element_type=F32)
    gates = jax.nn.softmax(logits, axis=1)
    dpick = dcomb * x_all[:, D + 2 : D + 5].astype(F32)
    dlogits = (gates * (dpick - jnp.sum(dpick * gates, axis=1, keepdims=True))).astype(BF16)
    d_router = lax.dot_general(dlogits, h2, TN, preferred_element_type=F32)
    dh2 = dh2[:, :D] + jnp.dot(dlogits, router, preferred_element_type=F32)
    d_ffn_gain = jnp.sum(dh2 * n2, axis=0, keepdims=True)
    g2 = dh2 * gain_two
    dx1 = diff + r2 * (g2 - n2 * jnp.mean(g2 * n2, axis=1, keepdims=True))
    da = dx1.astype(BF16)
    da_home = exchange(da)
    y_home = exchange(y.astype(BF16))

    sums = jnp.concatenate(
        [
            jnp.zeros((1, D), F32),
            d_ffn_gain,
            d_router,
            jnp.full((1, D), squares / (SEQ * 16), F32),
        ],
        axis=0,
    )
    sums = jnp.pad(sums, ((0, EXT - 6), (0, 0)))
    *dw_blocks, dqkv = call(
        attn_bwd_kernel,
        info,
        gather_group(da) + [wo, k, q, v, cos, sin, h1, mixed, w, after(lse, da_home, y_home), sums],
        [((4 * PART, SPLIT_A), BF16)] * 4
        + [((4 * PART, WA - SPLIT_A), BF16)] * 4
        + [((SEQ, QKV), BF16)],
        [
            ((D, HW), BF16),
            head,
            head,
            head,
            ((SEQ, HD), F32),
            ((SEQ, HD), F32),
            ((SEQ, D), BF16),
            head,
            ((D, WQ), BF16),
            ((SEQ, D), BF16),
            ((SEQ, HW), BF16),
            ((HW, SEQ), BF16),
            ((SEQ, HD), F32),
            ((SEQ, HD), F32),
            ((D, WA), BF16),
        ],
        6_000_000_000,
        LIM[5],
        far_in=range(8, 17),
        sems=9,
    )
    a, b = call(
        attn_in_kernel,
        info,
        [w, dqkv],
        [((512, D), BF16), ((512, D), BF16)],
        [((SEQ, D), BF16)],
        2_000_000_000,
        LIM[6],
    )
    x = tokens.astype(F32)
    to_z = sum_cores(a, b)
    first = (
        add_parts([after(dw_blocks[0], to_z)] + dw_blocks[1:4], along_y),
        add_parts([after(dw_blocks[4], to_z)] + dw_blocks[5:], along_x),
    )
    cuts = [slice(i * PART, (i + 1) * PART) for i in range(4)]
    dw = jnp.concatenate(
        [
            add_parts([first[0][cut] for cut in cuts], along_x),
            add_parts([first[1][cut] for cut in cuts], along_y),
        ],
        axis=1,
    )
    dwm_own = turn_home(after(dwm_own, first))
    dh1 = scatter_home(to_z)
    dw = lax.all_to_all(dw.reshape(8, n, WA), ("c", "z"), split_axis=0, concat_axis=0)
    dw = after(dw, dwm_own)
    d_qkv, d_out, d_gains, d_router, loss = call(
        finish_kernel,
        info,
        [dw],
        [((n, 3 * D), F32), ((n, D), F32), ((8, n), F32), ((n, 3), F32), ((1, 1), F32)],
        [],
        0,
        6,
    )

    r1 = lax.rsqrt(jnp.mean(x * x, axis=1, keepdims=True) + norm_eps)
    n1 = x * r1
    g1 = dh1 * ext[0:1, :]
    d_tokens = da_home.astype(F32) + r1 * (g1 - n1 * jnp.mean(g1 * n1, axis=1, keepdims=True))

    d_gu = dwm_own[:, :GU].reshape(-1, 4, 2, 128)[..., :UNITS].astype(F32)
    d_dn = dwm_own[:, GU:].reshape(-1, 4, 128)[..., :UNITS].astype(F32)
    return (
        y_home,
        loss.reshape(()),
        d_tokens,
        d_gains[0],
        d_qkv,
        d_out,
        d_router,
        d_gains[1],
        d_gu,
        d_dn,
    )


def solution(mesh):
    fine = Mesh(mesh.devices.reshape(4, 2, 2, 2, 4), ("y", "xl", "c", "xh", "z"))
    every = ("y", "xl", "c", "xh", "z")
    rows = P(every, None)
    in_specs = (
        rows,
        rows,
        P(),
        rows,
        P(every),
        rows,
        rows,
        rows,
        P(every),
        P(("y", "xl", "c"), None, None, ("xh", "z")),
        P(("y", "xl", "c"), None, ("xh", "z")),
    )
    out_specs = (
        rows,
        P(),
        rows,
        P(every),
        rows,
        rows,
        rows,
        P(every),
        P(("y", "xl", "c"), None, None, ("xh", "z")),
        P(("y", "xl", "c"), None, ("xh", "z")),
    )
    return jax.shard_map(
        on_device, mesh=fine, in_specs=in_specs, out_specs=out_specs, check_vma=False
    )
```

```python
import functools

import jax
import jax.numpy as jnp
import numpy as np
from jax import lax
from jax.experimental import pallas as pl
from jax.experimental.pallas import tpu as pltpu
from jax.sharding import Mesh, PartitionSpec as P

D = 1280
HD = 128
HEADS = 10
SLOTS = 2
GROUPS = 5
HW = SLOTS * HD
QKV = 3 * HW
EXT = 128
WQ = QKV + EXT
WA = WQ + HW
ROWS = 128
SEQ = 1024
UNITS = 112
GU = 4 * 2 * 128
DN = 4 * 128
WM = GU + DN
PART = 80
SPLIT_A = 640
SPLIT_M = 768
norm_eps = 1e-06
masked_score = -1e30
rope_base = 10000.0
SCALE = HD ** (-0.5)
LOG2E = float(np.log2(np.e))
SLOT = 3 * HD
F32 = jnp.float32
BF16 = jnp.bfloat16
MIB = 1024 * 1024
LIM = (52, 12, 10, 10, 12, 50, 10, 50)

NT = (((1,), (1,)), ((), ()))
TN = (((0,), (0,)), ((), ()))


def dot(a, b):
    return jnp.dot(a, b, preferred_element_type=F32)


def dot_nt(a, b):
    return lax.dot_general(a, b, NT, preferred_element_type=F32)


def dot_tn(a, b):
    return lax.dot_general(a, b, TN, preferred_element_type=F32)


def rows_of(start, count=ROWS):
    return pl.ds(pl.multiple_of(start, ROWS), count)


def half_turn(u):
    return pltpu.roll(u, HD // 2, 1)


def natural_rows(placed, out, first):
    half = PART // 2
    columns = slice(first, first + out.shape[1])
    for p in range(8):
        at = (p // 2 * 4 + p % 2) * PART
        low = placed[at : at + PART, columns].astype(F32)
        high = placed[at + 2 * PART : at + 3 * PART, columns].astype(F32)
        for i in range(2):
            cut = slice(i * half, (i + 1) * half)
            to = (2 * p + i) * PART
            out[to : to + PART, :] = jnp.concatenate([low[cut], high[cut]], axis=0).astype(BF16)


def place_kernel(info, *refs):
    x, chosen = refs[8:]
    for i in range(8):
        at = rows_of(info[i] * ROWS)
        x[at, :] = refs[i][:, :D]
        chosen[at, :] = refs[i][:, D:]


def masked(s, step, prefix):
    first = step * 256
    rest = s[first:]
    key = lax.broadcasted_iota(jnp.int32, rest.shape, 0)
    query = lax.broadcasted_iota(jnp.int32, rest.shape, 1)
    rest = jnp.where(key < jnp.maximum(query + 1, prefix - first), rest, masked_score)
    return rest if step == 0 else jnp.concatenate([s[:first], rest], axis=0)


def attn_fwd_kernel(info, w_far, x, cos, sin, *refs):
    saved = refs[:7]
    a, b, wext, lse, ext = refs[7:12]
    w, h1, q, k, v, mixed, wo, wp, vt, part, sems = refs[12:]
    held = [w, h1, q, k, v, mixed, wo]

    def keep(i):
        return pltpu.make_async_copy(held[i], saved[i], sems.at[i])

    load = pltpu.make_async_copy(w_far, wp, sems.at[7])
    load.start()
    load.wait()
    natural_rows(wp, w, 0)
    natural_rows(wp, wo, WQ)
    keep(0).start()
    keep(6).start()
    wext[...] = w[:, QKV:]
    ext_t = w[:, QKV:].astype(F32).T
    ext[...] = ext_t
    gain = ext_t[0:1, :]

    @pl.loop(0, 4)
    def _(step):
        at = rows_of(step * 256, 256)
        blk = x[at, :].astype(F32)
        r = lax.rsqrt(jnp.mean(blk * blk, axis=1, keepdims=True) + norm_eps)
        h = (blk * r * gain).astype(BF16)
        h1[at, :] = h
        full = dot(h, w[:, :QKV])
        c, s = cos[at, :], sin[at, :]
        for j in range(SLOTS):
            col = slice(j * HD, (j + 1) * HD)
            uq, uk, uv = (
                full[:, j * SLOT + i * HD : j * SLOT + (i + 1) * HD] for i in range(3)
            )
            q[at, col] = (uq * c + half_turn(uq) * s).astype(BF16)
            k[at, col] = (uk * c + half_turn(uk) * s).astype(BF16)
            v[at, col] = uv.astype(BF16)
            vt[col, at] = uv.T.astype(BF16)

    for i in range(1, 5):
        keep(i).start()
    lse[...] = jnp.zeros_like(lse)
    for j in range(SLOTS):
        col = slice(j * HD, (j + 1) * HD)
        for step in range(4):
            at = slice(step * 256, (step + 1) * 256)
            s = masked(dot_nt(k[:, col], q[at, col]), step, info[16])
            top = jnp.max(s, axis=0, keepdims=True)
            e = jnp.exp2((s - top) * (SCALE * LOG2E))
            total = jnp.sum(e, axis=0, keepdims=True)
            mix = dot(vt[col, :], e.astype(BF16)) * (1.0 / total)
            mixed[at, col] = mix.T.astype(BF16)
            lse[j : j + 1, at] = top * (SCALE * LOG2E) + jnp.log2(total)

    keep(5).start()

    @pl.loop(0, 4)
    def _(step):
        at = rows_of(step * 256, 256)
        part[at, :] = dot_nt(mixed[at, :], wo[...]).astype(BF16)

    give_blocks(info, part, a, b)
    for i in range(7):
        keep(i).wait()


def give_blocks(info, part, a, b):
    for i in range(4):
        out = slice(i * ROWS, (i + 1) * ROWS)
        a[out, :] = part[rows_of(info[8 + i] * ROWS), :]
        b[out, :] = part[rows_of(info[12 + i] * ROWS), :]


def moe_fwd_kernel(info, *refs):
    hs = refs[:8]
    wm, wext, chosen = refs[8:11]
    a, b, h2, gu, z, comb = refs[11:17]
    (part,) = refs[17:]
    for i in range(8):
        h2[rows_of(info[i] * ROWS), :] = hs[i][...]

    @pl.loop(0, 4)
    def _(step):
        at = rows_of(step * 256, 256)
        h = h2[at, :]
        logits = dot(h, wext[...])
        lane = lax.broadcasted_iota(jnp.int32, logits.shape, 1)
        live = (lane >= 2) & (lane < 5)
        logits = jnp.where(live, logits, masked_score)
        e = jnp.exp(logits - jnp.max(logits, axis=1, keepdims=True))
        gates = e / jnp.sum(e, axis=1, keepdims=True)
        cb = gates * chosen[at, :].astype(F32)
        comb[at, :] = cb
        full = dot(h, wm[:, :GU])
        gu[at, :] = full
        for x in range(4):
            gate = full[:, x * 256 : x * 256 + 128]
            up = full[:, x * 256 + 128 : x * 256 + 256]
            act = gate * jax.nn.sigmoid(gate) * up
            if x:
                act = act * cb[:, x + 1 : x + 2]
            z[at, x * 128 : (x + 1) * 128] = act.astype(BF16)
        part[at, :] = dot_nt(z[at, :], wm[:, GU:]).astype(BF16)

    give_blocks(info, part, a, b)


def moe_bwd_kernel(info, *refs):
    ds = refs[:8]
    wm, gu, comb = refs[8:11]
    a, b, dm, dgu = refs[11:15]
    (part,) = refs[15:]
    for i in range(8):
        dm[rows_of(info[i] * ROWS), :] = ds[i][...]

    @pl.loop(0, 4)
    def _(step):
        at = rows_of(step * 256, 256)
        dz = dot(dm[at, :], wm[:, GU:])
        cb = comb[at, :]
        lane = lax.broadcasted_iota(jnp.int32, (256, 128), 1)
        extra = jnp.zeros((256, 128), F32)
        for x in range(4):
            gate = gu[at, x * 256 : x * 256 + 128]
            up = gu[at, x * 256 + 128 : x * 256 + 256]
            sig = jax.nn.sigmoid(gate)
            silu = gate * sig
            dact = dz[:, x * 128 : (x + 1) * 128]
            if x:
                dc = jnp.sum(dact * (silu * up), axis=1, keepdims=True)
                high = dc.astype(BF16).astype(F32)
                extra = jnp.where(lane == x + 1, high, extra)
                extra = jnp.where(lane == x + 4, dc - high, extra)
                dact = dact * cb[:, x + 1 : x + 2]
            dgu[at, x * 256 : x * 256 + 128] = (
                dact * up * sig * (1.0 + gate * (1.0 - sig))
            ).astype(BF16)
            dgu[at, x * 256 + 128 : x * 256 + 256] = (dact * silu).astype(BF16)
        part[at, :D] = dot_nt(dgu[at, :], wm[:, :GU]).astype(BF16)
        part[at, D:] = extra.astype(BF16)

    give_blocks(info, part, a, b)


def moe_grad_kernel(info, *refs):
    h2, dgu, dm, z, saved, rows, sems = refs

    def keep(i):
        cut = slice(i * 640, (i + 1) * 640)
        return pltpu.make_async_copy(rows.at[cut, :], saved.at[cut, :], sems.at[i])

    for i in range(2):
        cut = slice(i * 640, (i + 1) * 640)
        rows[cut, :GU] = dot_tn(h2[:, cut], dgu[...]).astype(BF16)
        rows[cut, GU:] = dot_tn(dm[:, cut], z[...]).astype(BF16)
        keep(i).start()
    for i in range(2):
        keep(i).wait()


def slot_bwd(j, info, k, q, v, dm, mixed, lse, cos, sin, dqkv, kt, dk, dv):
    kt[...] = k[...].astype(F32).T.astype(BF16)
    for step in range(4):
        at = slice(step * 256, (step + 1) * 256)
        qb, dmb = q[at, :], dm[at, :]
        s = masked(dot_nt(k[...], qb), step, info[16])
        p = jnp.exp2(s * (SCALE * LOG2E) - lse[j : j + 1, at])
        more = dot(p.astype(BF16), dmb)
        dv[...] = more if step == 0 else dv[...] + more
        delta = jnp.sum((dmb.astype(F32) * mixed[at, :].astype(F32)).T, axis=0, keepdims=True)
        ds = (p * (dot_nt(v[...], dmb) - delta)).astype(BF16)
        more = dot(ds, qb)
        dk[...] = more if step == 0 else dk[...] + more
        dq = dot(kt[...], ds).T * SCALE
        dqkv[at, :HD] = (dq * cos[at, :] - half_turn(dq) * sin[at, :]).astype(BF16)
    u = dk[...] * SCALE
    dqkv[:, HD : 2 * HD] = (u * cos[...] - half_turn(u) * sin[...]).astype(BF16)
    dqkv[:, 2 * HD :] = dv[...].astype(BF16)


def to_places(full, i, rows):
    half = PART // 2
    for p in range(4):
        for g in range(2):
            top = p * 2 * PART + g * half
            to = i * 640 + (p * 2 + g) * PART
            rows[to : to + PART, :] = jnp.concatenate(
                [full[top : top + half], full[top + PART : top + PART + half]], axis=0
            ).astype(BF16)


def pick_y(info, rows, outs):
    for j in range(4):
        for m in range(4):
            at = pl.ds(pl.multiple_of(info[32 + j * 4 + m], 16), PART)
            outs[j][m * PART : (m + 1) * PART, :] = rows[at, :]


def pick_x(info, rows, outs):
    for j in range(4):
        for m in range(4):
            at = pl.ds(pl.multiple_of(info[32 + j * 4 + m], 16), PART)
            outs[m][j * PART : (j + 1) * PART, :] = rows[at, :]


def head_loads(j, far, near, sems):
    col = slice(j * HD, (j + 1) * HD)
    return [
        pltpu.make_async_copy(a.at[:, col], b, sems.at[i])
        for i, (a, b) in enumerate(zip(far, near))
    ]


def attn_bwd_kernel(info, *refs):
    ds = refs[:8]
    wo_far, k_far, q_far, v_far, mixed_far, h1_far, w_far, cos, sin, lse = refs[8:18]
    outs = refs[18:22]
    dqkv, dm1, gain = refs[22:25]
    k, q, v, wo, mixed, h1, w, da, dm0, kt, dk, dv, rows, sems = refs[25:]
    loads = [
        pltpu.make_async_copy(wo_far, wo, sems.at[3]),
        pltpu.make_async_copy(mixed_far, mixed, sems.at[4]),
        pltpu.make_async_copy(h1_far, h1, sems.at[5]),
        pltpu.make_async_copy(w_far.at[:, :SLOT], w, sems.at[6]),
    ]
    loads[0].start()
    heads = head_loads(0, (k_far, q_far, v_far), (k, q, v), sems)
    for load in heads + loads[1:]:
        load.start()
    for i in range(8):
        da[rows_of(info[i] * ROWS), :] = ds[i][...]
    loads[0].wait()

    @pl.loop(0, 4)
    def _(step):
        at = rows_of(step * 256, 256)
        dmix = dot(da[at, :], wo[...]).astype(BF16)
        dm0[at, :] = dmix[:, :HD]
        dm1[at, :] = dmix[:, HD:]

    for load in heads + loads[1:2]:
        load.wait()
    slot_bwd(0, info, k, q, v, dm0, mixed.at[:, :HD], lse, cos, sin, dqkv, kt, dk, dv)
    for load in loads[2:]:
        load.wait()
    for i in range(2):
        cut = slice(i * 640, (i + 1) * 640)
        dw = dot_tn(h1[:, cut], dqkv[...])
        gain[cut, :] = jnp.sum(dw * w[cut, :].astype(F32), axis=1, keepdims=True)
        do = dot_tn(da[:, cut], mixed[...])
        to_places(jnp.concatenate([dw, do], axis=1), i, rows)
    pick_y(info, rows, outs)


def attn_bwd_second_kernel(info, *refs):
    dm, k_far, q_far, v_far, mixed_far, h1_far, w_far, cos, sin, lse, gain, sums = refs[:12]
    outs = refs[12:16]
    dqkv = refs[16]
    k, q, v, mixed, h1, w, kt, dk, dv, rows, sems = refs[17:]
    loads = [
        pltpu.make_async_copy(h1_far, h1, sems.at[5]),
        pltpu.make_async_copy(w_far.at[:, SLOT:], w, sems.at[6]),
    ]
    heads = head_loads(1, (k_far, q_far, v_far, mixed_far), (k, q, v, mixed), sems)
    for load in heads + loads:
        load.start()
    for load in heads:
        load.wait()
    slot_bwd(1, info, k, q, v, dm, mixed, lse, cos, sin, dqkv, kt, dk, dv)
    for load in loads:
        load.wait()
    for i in range(2):
        cut = slice(i * 640, (i + 1) * 640)
        dw = dot_tn(h1[:, cut], dqkv[...])
        both = gain[cut, :] + jnp.sum(dw * w[cut, :SLOT].astype(F32), axis=1, keepdims=True)
        extra = sums[:, cut].T
        lane = lax.broadcasted_iota(jnp.int32, extra.shape, 1)
        extra = jnp.where(lane == 0, both / w[cut, SLOT : SLOT + 1].astype(F32), extra)
        to_places(jnp.concatenate([dw, extra], axis=1), i, rows)
    pick_x(info, rows, outs)


def attn_in_kernel(info, *refs):
    w, dq0, dq1, a, b, part = refs

    @pl.loop(0, 4)
    def _(step):
        at = rows_of(step * 256, 256)
        both = jnp.concatenate([dq0[at, :], dq1[at, :]], axis=1)
        part[at, :] = dot_nt(both, w[:, :QKV]).astype(BF16)

    give_blocks(info, part, a, b)


def finish_kernel(info, dw, qkv, out, gains, router, loss):
    for g in range(GROUPS):
        for j in range(SLOTS):
            for part in range(3):
                to = part * D + g * HW + j * HD
                at = j * SPLIT_A + part * HD
                qkv[:, to : to + HD] = dw[g, :, at : at + HD].astype(F32)
        out[:, g * HW : (g + 1) * HW] = dw[g, :, SLOT:SPLIT_A].astype(F32)
    last = slice(SPLIT_A + SLOT, WA)
    total = dw[0, :, last].astype(F32)
    for g in range(1, 8):
        total = total + dw[g, :, last].astype(F32)
    router[...] = total[:, 2:5]
    loss[...] = total[0:1, 5:6]
    gains[...] = total.T[0:8, :]


def call(kernel, info, args, outs, scratch, flops, mib, far_in=(), far_out=(), sems=0):
    total = sum(int(np.prod(x.shape)) * x.dtype.itemsize for x in args)
    total += sum(int(np.prod(s)) * jnp.dtype(t).itemsize for s, t in outs)

    def spec(far):
        return pl.BlockSpec(memory_space=pltpu.HBM if far else pltpu.VMEM)

    return pl.pallas_call(
        kernel,
        out_shape=[jax.ShapeDtypeStruct(s, t) for s, t in outs],
        in_specs=[pl.BlockSpec(memory_space=pltpu.SMEM)]
        + [spec(i in far_in) for i in range(len(args))],
        out_specs=[spec(i in far_out) for i in range(len(outs))],
        scratch_shapes=[pltpu.VMEM(s, t) for s, t in scratch]
        + ([pltpu.SemaphoreType.DMA((sems,))] if sems else []),
        compiler_params=pltpu.CompilerParams(vmem_limit_bytes=mib * MIB),
        cost_estimate=pl.CostEstimate(flops=flops, bytes_accessed=total, transcendentals=0),
    )(info, *args)


def exchange(x):
    return lax.ppermute(x, ("c", "xh"), [(0, 0), (1, 2), (2, 1), (3, 3)])


def turn_out(x):
    pairs = [(i * 4 + j * 2 + k, j * 4 + k * 2 + i) for i in (0, 1) for j in (0, 1) for k in (0, 1)]
    return lax.ppermute(x, ("xl", "c", "xh"), pairs)


def turn_home(x):
    pairs = [(j * 4 + k * 2 + i, i * 4 + j * 2 + k) for i in (0, 1) for j in (0, 1) for k in (0, 1)]
    return lax.ppermute(x, ("xl", "c", "xh"), pairs)


def along_z(x, k):
    return lax.ppermute(x, "z", [(i, (i + k) % 4) for i in range(4)])


def along_y(x, k):
    return lax.ppermute(x, "y", [(i, (i + k) % 4) for i in range(4)])


def along_x(x, k):
    place = [0, 2, 1, 3]
    return lax.ppermute(x, ("xl", "xh"), [(place[i], place[(i + k) % 4]) for i in range(4)])


def after(x, *deps):
    return lax.optimization_barrier((x, deps))[0]


def add_parts(parts, move):
    total = parts[0].astype(F32)
    for k in (1, 2, 3):
        total = total + move(parts[k], k).astype(F32)
    return total.astype(BF16)


def to_other_core(x):
    return lax.ppermute(x, "c", [(0, 1), (1, 0)])


def gather_group(x, *deps):
    own = [x] + [along_z(x, k) for k in (1, 2, 3)]
    last = after(own[3], *deps) if deps else own[3]
    return own + [to_other_core(part) for part in own[:3] + [last]]


def scatter_group(a, b):
    got = to_other_core(b)
    s = [
        (a[i * ROWS : (i + 1) * ROWS].astype(F32) + got[i * ROWS : (i + 1) * ROWS].astype(F32))
        for i in range(4)
    ]
    total = s[0]
    for k in (1, 2, 3):
        total = total + along_z(s[k].astype(BF16), k).astype(F32)
    return total


def sum_cores(a, b):
    got = to_other_core(b)
    cuts = [slice(k * ROWS, (k + 1) * ROWS) for k in range(4)]
    return [(a[cut].astype(F32) + got[cut].astype(F32)).astype(BF16) for cut in cuts]


def scatter_home(parts):
    total = 0.0
    for k in range(4):
        pairs = [
            (c * 8 + x * 4 + z, x * 8 + c * 4 + (z + k) % 4)
            for c in range(2)
            for x in range(2)
            for z in range(4)
        ]
        total = total + lax.ppermute(parts[k], ("c", "xh", "z"), pairs).astype(F32)
    return total


PLANE = ("y", "xl", "xh")
RING = ("y", "xh", "xl")


def rope_tables():
    places = jnp.arange(SEQ, dtype=jnp.int32).astype(F32)
    half = HD // 2
    speeds = rope_base ** (-jnp.arange(half, dtype=F32) / half)
    angles = places[:, None] * speeds[None, :]
    c, s = jnp.cos(angles), jnp.sin(angles)
    return jnp.concatenate([c, c], axis=1), jnp.concatenate([-s, s], axis=1)


def on_device(
    tokens, teacher, prefix, routes, attn_gain, w_qkv, w_out, router_w, ffn_gain, w_gate_up, w_down
):
    core, zz = lax.axis_index("c"), lax.axis_index("z")
    near = [core * 4 + (zz + k) % 4 for k in range(4)]
    far = [(1 - core) * 4 + (zz + k) % 4 for k in range(4)]
    back = [0, 3, 2, 1]
    sequence = lax.axis_index(PLANE)
    yy = lax.axis_index("y")
    xx = lax.axis_index("xh") * 2 + lax.axis_index("xl")

    def place(dy, dx):
        y, x = (yy + dy) % 4, (xx + dx) % 4
        return (y * 4 + x % 2 * 2 + x // 2) * PART

    info = jnp.stack(
        [near[i] for i in back]
        + [far[i] for i in back]
        + near
        + far
        + [prefix[sequence]]
        + [jnp.int32(0)] * 15
        + [place(j, m) for j in range(4) for m in range(4)]
    ).astype(jnp.int32)

    lanes = jnp.arange(EXT, dtype=jnp.int32)[None, :]
    chosen = (routes[:, 0:1] + 2 == lanes) | (routes[:, 1:2] + 2 == lanes)
    x_all = exchange(jnp.concatenate([tokens, chosen.astype(BF16)], axis=1))
    small = jnp.concatenate([attn_gain[:, None], ffn_gain[:, None], router_w], axis=1)
    raw = jnp.concatenate([w_qkv, w_out, jnp.pad(small, ((0, 0), (0, EXT - 5)))], axis=1)
    n = raw.shape[0]
    heads = raw[:, : 3 * D].reshape(n, 3, GROUPS, SLOTS, HD).transpose(2, 0, 3, 1, 4)
    outs = raw[:, 3 * D : 4 * D].reshape(n, GROUPS, HW).transpose(1, 0, 2)
    extra = jnp.broadcast_to(raw[None, :, 4 * D :], (8, n, EXT))
    none = ((0, 8 - GROUPS), (0, 0), (0, 0))
    packed = jnp.concatenate(
        [jnp.pad(heads.reshape(GROUPS, n, QKV), none), extra, jnp.pad(outs, none)], axis=2
    )
    packed = lax.all_to_all(packed, ("c", "z"), split_axis=0, concat_axis=0).reshape(8 * n, WA)
    lane_pad = 128 - UNITS
    wm_own = jnp.concatenate(
        [
            jnp.pad(w_gate_up, ((0, 0), (0, 0), (0, 0), (0, lane_pad))).reshape(-1, GU),
            jnp.pad(w_down, ((0, 0), (0, 0), (0, lane_pad))).reshape(-1, DN),
        ],
        axis=1,
    )
    wm_own = turn_out(wm_own)
    w_all = lax.all_gather(packed, RING, axis=0, tiled=True)
    x_seq, chosen_all = call(
        place_kernel,
        info,
        gather_group(x_all),
        [((SEQ, D), BF16), ((SEQ, EXT), BF16)],
        [],
        0,
        6,
    )
    wm = lax.all_gather(after(wm_own, w_all, x_seq), RING, axis=0, tiled=True)
    teach = exchange(teacher)
    cos, sin = rope_tables()

    head = ((SEQ, HW), BF16)
    w, h1, q, k, v, mixed, wo, a, b, wext, lse, ext = call(
        attn_fwd_kernel,
        info,
        [w_all, x_seq, cos, sin],
        [
            ((D, WQ), BF16),
            ((SEQ, D), BF16),
            head,
            head,
            head,
            head,
            ((D, HW), BF16),
            ((512, D), BF16),
            ((512, D), BF16),
            ((D, EXT), BF16),
            ((8, SEQ), F32),
            ((EXT, D), F32),
        ],
        [
            ((D, WQ), BF16),
            ((SEQ, D), BF16),
            head,
            head,
            head,
            head,
            ((D, HW), BF16),
            ((D, WA), BF16),
            ((HW, SEQ), BF16),
            ((SEQ, D), BF16),
        ],
        5_000_000_000,
        LIM[0],
        far_in=(0,),
        far_out=range(7),
        sems=8,
    )
    x = x_all[:, :D].astype(F32)
    x1 = x + scatter_group(a, b)
    r2 = lax.rsqrt(jnp.mean(x1 * x1, axis=1, keepdims=True) + norm_eps)
    n2 = x1 * r2
    gain_two = ext[1:2, :]
    h2 = (n2 * gain_two).astype(BF16)

    a, b, h2_all, gu, z, comb = call(
        moe_fwd_kernel,
        info,
        gather_group(h2, wm) + [wm, wext, chosen_all],
        [
            ((512, D), BF16),
            ((512, D), BF16),
            ((SEQ, D), BF16),
            ((SEQ, GU), F32),
            ((SEQ, DN), BF16),
            ((SEQ, EXT), F32),
        ],
        [((SEQ, D), BF16)],
        4_000_000_000,
        LIM[2],
    )
    y = x1 + scatter_group(a, b)
    diff = y - teach.astype(F32)
    squares = jnp.sum(diff * diff)
    dm = diff.astype(BF16)
    a, b, dm_all, dgu = call(
        moe_bwd_kernel,
        info,
        gather_group(dm) + [wm, gu, comb],
        [((512, D + EXT), BF16), ((512, D + EXT), BF16), ((SEQ, D), BF16), ((SEQ, GU), BF16)],
        [((SEQ, D + EXT), BF16)],
        4_000_000_000,
        LIM[3],
    )
    (dwm,) = call(
        moe_grad_kernel,
        info,
        [h2_all, dgu, dm_all, z],
        [((D, WM), BF16)],
        [((D, WM), BF16)],
        4_000_000_000,
        LIM[4],
        far_out=(0,),
        sems=2,
    )
    dwm_own = lax.psum_scatter(dwm, RING, scatter_dimension=0, tiled=True)
    dh2 = scatter_group(a, b)
    dcomb = dh2[:, D + 2 : D + 5] + dh2[:, D + 5 : D + 8]
    router = ext[2:5, :].astype(BF16)
    logits = lax.dot_general(h2, router, NT, preferred_element_type=F32)
    gates = jax.nn.softmax(logits, axis=1)
    dpick = dcomb * x_all[:, D + 2 : D + 5].astype(F32)
    dlogits = (gates * (dpick - jnp.sum(dpick * gates, axis=1, keepdims=True))).astype(BF16)
    d_router = lax.dot_general(dlogits, h2, TN, preferred_element_type=F32)
    dh2 = dh2[:, :D] + jnp.dot(dlogits, router, preferred_element_type=F32)
    d_ffn_gain = jnp.sum(dh2 * n2, axis=0, keepdims=True)
    g2 = dh2 * gain_two
    dx1 = diff + r2 * (g2 - n2 * jnp.mean(g2 * n2, axis=1, keepdims=True))
    da = dx1.astype(BF16)
    da_home = exchange(da)
    y_home = exchange(y.astype(BF16))

    sums = jnp.concatenate(
        [
            jnp.zeros((1, D), F32),
            d_ffn_gain,
            d_router,
            jnp.full((1, D), squares / (SEQ * 16), F32),
        ],
        axis=0,
    )
    sums = jnp.pad(sums, ((0, EXT - 6), (0, 0)))
    one = ((SEQ, HD), BF16)
    *a_blocks, dq0, dm1, gain = call(
        attn_bwd_kernel,
        info,
        gather_group(da)
        + [wo, k, q, v, mixed, h1, w, cos, sin, after(lse, da_home, y_home)],
        [((4 * PART, SPLIT_A), BF16)] * 4 + [((SEQ, SLOT), BF16), one, ((D, 1), F32)],
        [
            one,
            one,
            one,
            ((D, HW), BF16),
            head,
            ((SEQ, D), BF16),
            ((D, SLOT), BF16),
            ((SEQ, D), BF16),
            one,
            ((HD, SEQ), BF16),
            ((SEQ, HD), F32),
            ((SEQ, HD), F32),
            ((D, SPLIT_A), BF16),
        ],
        5_000_000_000,
        LIM[5],
        far_in=range(8, 15),
        sems=7,
    )
    *b_blocks, dq1 = call(
        attn_bwd_second_kernel,
        info,
        [dm1, k, q, v, mixed, h1, w, cos, sin, lse, gain, sums],
        [((4 * PART, WA - SPLIT_A), BF16)] * 4 + [((SEQ, SLOT), BF16)],
        [
            one,
            one,
            one,
            one,
            ((SEQ, D), BF16),
            ((D, SLOT + EXT), BF16),
            ((HD, SEQ), BF16),
            ((SEQ, HD), F32),
            ((SEQ, HD), F32),
            ((D, WA - SPLIT_A), BF16),
        ],
        3_000_000_000,
        LIM[7],
        far_in=range(1, 7),
        sems=7,
    )
    a, b = call(
        attn_in_kernel,
        info,
        [w, dq0, dq1],
        [((512, D), BF16), ((512, D), BF16)],
        [((SEQ, D), BF16)],
        2_000_000_000,
        LIM[6],
    )
    x = tokens.astype(F32)
    to_z = sum_cores(a, b)
    first = (
        add_parts([after(a_blocks[0], to_z)] + a_blocks[1:], along_y),
        add_parts([after(b_blocks[0], to_z)] + b_blocks[1:], along_x),
    )
    dwm_own = turn_home(after(dwm_own, first))
    cuts = [slice(i * PART, (i + 1) * PART) for i in range(4)]
    dw = jnp.concatenate(
        [
            add_parts([first[0][cut] for cut in cuts], along_x),
            add_parts([first[1][cut] for cut in cuts], along_y),
        ],
        axis=1,
    )
    dh1 = scatter_home(to_z)
    dw = lax.all_to_all(dw.reshape(8, n, WA), ("c", "z"), split_axis=0, concat_axis=0)
    dw = after(dw, dwm_own)
    d_qkv, d_out, d_gains, d_router, loss = call(
        finish_kernel,
        info,
        [dw],
        [((n, 3 * D), F32), ((n, D), F32), ((8, n), F32), ((n, 3), F32), ((1, 1), F32)],
        [],
        0,
        6,
    )

    r1 = lax.rsqrt(jnp.mean(x * x, axis=1, keepdims=True) + norm_eps)
    n1 = x * r1
    g1 = dh1 * ext[0:1, :]
    d_tokens = da_home.astype(F32) + r1 * (g1 - n1 * jnp.mean(g1 * n1, axis=1, keepdims=True))

    d_gu = dwm_own[:, :GU].reshape(-1, 4, 2, 128)[..., :UNITS].astype(F32)
    d_dn = dwm_own[:, GU:].reshape(-1, 4, 128)[..., :UNITS].astype(F32)
    return (
        y_home,
        loss.reshape(()),
        d_tokens,
        d_gains[0],
        d_qkv,
        d_out,
        d_router,
        d_gains[1],
        d_gu,
        d_dn,
    )


def solution(mesh):
    fine = Mesh(mesh.devices.reshape(4, 2, 2, 2, 4), ("y", "xl", "c", "xh", "z"))
    every = ("y", "xl", "c", "xh", "z")
    rows = P(every, None)
    in_specs = (
        rows,
        rows,
        P(),
        rows,
        P(every),
        rows,
        rows,
        rows,
        P(every),
        P(("y", "xl", "c"), None, None, ("xh", "z")),
        P(("y", "xl", "c"), None, ("xh", "z")),
    )
    out_specs = (
        rows,
        P(),
        rows,
        P(every),
        rows,
        rows,
        rows,
        P(every),
        P(("y", "xl", "c"), None, None, ("xh", "z")),
        P(("y", "xl", "c"), None, ("xh", "z")),
    )
    return jax.shard_map(
        on_device, mesh=fine, in_specs=in_specs, out_specs=out_specs, check_vma=False
    )
```

```python
import functools

import jax
import jax.numpy as jnp
import numpy as np
from jax import lax
from jax.experimental import pallas as pl
from jax.experimental.pallas import tpu as pltpu
from jax.sharding import Mesh, PartitionSpec as P

D = 1280
HD = 128
HEADS = 10
SLOTS = 2
GROUPS = 5
HW = SLOTS * HD
QKV = 3 * HW
EXT = 128
WQ = QKV + EXT
WA = WQ + HW
ROWS = 128
SEQ = 1024
UNITS = 112
GU = 4 * 2 * 128
DN = 4 * 128
WM = GU + DN
PART = 80
SPLIT_A = 640
SPLIT_M = 768
norm_eps = 1e-06
masked_score = -1e30
rope_base = 10000.0
SCALE = HD ** (-0.5)
LOG2E = float(np.log2(np.e))
SLOT = 3 * HD
F32 = jnp.float32
BF16 = jnp.bfloat16
MIB = 1024 * 1024
LIM = (52, 12, 10, 10, 12, 50, 10, 50)

NT = (((1,), (1,)), ((), ()))
TN = (((0,), (0,)), ((), ()))


def dot(a, b):
    return jnp.dot(a, b, preferred_element_type=F32)


def dot_nt(a, b):
    return lax.dot_general(a, b, NT, preferred_element_type=F32)


def dot_tn(a, b):
    return lax.dot_general(a, b, TN, preferred_element_type=F32)


def rows_of(start, count=ROWS):
    return pl.ds(pl.multiple_of(start, ROWS), count)


def half_turn(u):
    return pltpu.roll(u, HD // 2, 1)


def natural_rows(placed, out, first):
    half = PART // 2
    columns = slice(first, first + out.shape[1])
    for p in range(8):
        at = (p // 2 * 4 + p % 2) * PART
        low = placed[at : at + PART, columns].astype(F32)
        high = placed[at + 2 * PART : at + 3 * PART, columns].astype(F32)
        for i in range(2):
            cut = slice(i * half, (i + 1) * half)
            to = (2 * p + i) * PART
            out[to : to + PART, :] = jnp.concatenate([low[cut], high[cut]], axis=0).astype(BF16)


def place_kernel(info, *refs):
    x, chosen = refs[8:]
    for i in range(8):
        at = rows_of(info[i] * ROWS)
        x[at, :] = refs[i][:, :D]
        chosen[at, :] = refs[i][:, D:]


def masked(s, step, prefix):
    first = step * 256
    rest = s[first:]
    key = lax.broadcasted_iota(jnp.int32, rest.shape, 0)
    query = lax.broadcasted_iota(jnp.int32, rest.shape, 1)
    rest = jnp.where(key < jnp.maximum(query + 1, prefix - first), rest, masked_score)
    return rest if step == 0 else jnp.concatenate([s[:first], rest], axis=0)


def attn_fwd_kernel(info, w_far, x, cos, sin, *refs):
    saved = refs[:7]
    a, b, wext, lse, ext = refs[7:12]
    w, h1, q, k, v, mixed, wo, wp, vt, part, sems = refs[12:]
    held = [w, h1, q, k, v, mixed, wo]

    def keep(i):
        return pltpu.make_async_copy(held[i], saved[i], sems.at[i])

    load = pltpu.make_async_copy(w_far, wp, sems.at[7])
    load.start()
    load.wait()
    natural_rows(wp, w, 0)
    natural_rows(wp, wo, WQ)
    keep(0).start()
    keep(6).start()
    wext[...] = w[:, QKV:]
    ext_t = w[:, QKV:].astype(F32).T
    ext[...] = ext_t
    gain = ext_t[0:1, :]

    @pl.loop(0, 4)
    def _(step):
        at = rows_of(step * 256, 256)
        blk = x[at, :].astype(F32)
        r = lax.rsqrt(jnp.mean(blk * blk, axis=1, keepdims=True) + norm_eps)
        h = (blk * r * gain).astype(BF16)
        h1[at, :] = h
        full = dot(h, w[:, :QKV])
        c, s = cos[at, :], sin[at, :]
        for j in range(SLOTS):
            col = slice(j * HD, (j + 1) * HD)
            uq, uk, uv = (
                full[:, j * SLOT + i * HD : j * SLOT + (i + 1) * HD] for i in range(3)
            )
            q[at, col] = (uq * c + half_turn(uq) * s).astype(BF16)
            k[at, col] = (uk * c + half_turn(uk) * s).astype(BF16)
            v[at, col] = uv.astype(BF16)
            vt[col, at] = uv.T.astype(BF16)

    for i in range(1, 5):
        keep(i).start()
    lse[...] = jnp.zeros_like(lse)
    for j in range(SLOTS):
        col = slice(j * HD, (j + 1) * HD)
        for step in range(4):
            at = slice(step * 256, (step + 1) * 256)
            s = masked(dot_nt(k[:, col], q[at, col]), step, info[16])
            top = jnp.max(s, axis=0, keepdims=True)
            e = jnp.exp2((s - top) * (SCALE * LOG2E))
            total = jnp.sum(e, axis=0, keepdims=True)
            mix = dot(vt[col, :], e.astype(BF16)) * (1.0 / total)
            mixed[at, col] = mix.T.astype(BF16)
            lse[j : j + 1, at] = top * (SCALE * LOG2E) + jnp.log2(total)

    keep(5).start()

    @pl.loop(0, 4)
    def _(step):
        at = rows_of(step * 256, 256)
        part[at, :] = dot_nt(mixed[at, :], wo[...]).astype(BF16)

    give_blocks(info, part, a, b)
    for i in range(7):
        keep(i).wait()


def give_blocks(info, part, a, b):
    for i in range(4):
        out = slice(i * ROWS, (i + 1) * ROWS)
        a[out, :] = part[rows_of(info[8 + i] * ROWS), :]
        b[out, :] = part[rows_of(info[12 + i] * ROWS), :]


def moe_fwd_kernel(info, *refs):
    hs = refs[:8]
    wm, wext, chosen = refs[8:11]
    a, b, h2, gu, z, comb = refs[11:17]
    (part,) = refs[17:]
    for i in range(8):
        h2[rows_of(info[i] * ROWS), :] = hs[i][...]

    @pl.loop(0, 4, unroll=True)
    def _(step):
        at = rows_of(step * 256, 256)
        h = h2[at, :]
        logits = dot(h, wext[...])
        lane = lax.broadcasted_iota(jnp.int32, logits.shape, 1)
        live = (lane >= 2) & (lane < 5)
        logits = jnp.where(live, logits, masked_score)
        e = jnp.exp(logits - jnp.max(logits, axis=1, keepdims=True))
        gates = e / jnp.sum(e, axis=1, keepdims=True)
        cb = gates * chosen[at, :].astype(F32)
        comb[at, :] = cb
        full = dot(h, wm[:, :GU])
        gu[at, :] = full
        for x in range(4):
            gate = full[:, x * 256 : x * 256 + 128]
            up = full[:, x * 256 + 128 : x * 256 + 256]
            act = gate * jax.nn.sigmoid(gate) * up
            if x:
                act = act * cb[:, x + 1 : x + 2]
            z[at, x * 128 : (x + 1) * 128] = act.astype(BF16)
        part[at, :] = dot_nt(z[at, :], wm[:, GU:]).astype(BF16)

    give_blocks(info, part, a, b)


def moe_bwd_kernel(info, *refs):
    ds = refs[:8]
    wm, gu, comb = refs[8:11]
    a, b, dm, dgu = refs[11:15]
    (part,) = refs[15:]
    for i in range(8):
        dm[rows_of(info[i] * ROWS), :] = ds[i][...]

    @pl.loop(0, 4, unroll=True)
    def _(step):
        at = rows_of(step * 256, 256)
        dz = dot(dm[at, :], wm[:, GU:])
        cb = comb[at, :]
        lane = lax.broadcasted_iota(jnp.int32, (256, 128), 1)
        extra = jnp.zeros((256, 128), F32)
        for x in range(4):
            gate = gu[at, x * 256 : x * 256 + 128]
            up = gu[at, x * 256 + 128 : x * 256 + 256]
            sig = jax.nn.sigmoid(gate)
            silu = gate * sig
            dact = dz[:, x * 128 : (x + 1) * 128]
            if x:
                dc = jnp.sum(dact * (silu * up), axis=1, keepdims=True)
                high = dc.astype(BF16).astype(F32)
                extra = jnp.where(lane == x + 1, high, extra)
                extra = jnp.where(lane == x + 4, dc - high, extra)
                dact = dact * cb[:, x + 1 : x + 2]
            dgu[at, x * 256 : x * 256 + 128] = (
                dact * up * sig * (1.0 + gate * (1.0 - sig))
            ).astype(BF16)
            dgu[at, x * 256 + 128 : x * 256 + 256] = (dact * silu).astype(BF16)
        part[at, :D] = dot_nt(dgu[at, :], wm[:, :GU]).astype(BF16)
        part[at, D:] = extra.astype(BF16)

    give_blocks(info, part, a, b)


def moe_grad_kernel(info, *refs):
    h2, dgu, dm, z, saved, rows, sems = refs

    def keep(i):
        cut = slice(i * 640, (i + 1) * 640)
        return pltpu.make_async_copy(rows.at[cut, :], saved.at[cut, :], sems.at[i])

    for i in range(2):
        cut = slice(i * 640, (i + 1) * 640)
        rows[cut, :GU] = dot_tn(h2[:, cut], dgu[...]).astype(BF16)
        rows[cut, GU:] = dot_tn(dm[:, cut], z[...]).astype(BF16)
        keep(i).start()
    for i in range(2):
        keep(i).wait()


def slot_bwd(j, info, k, q, v, dm, mixed, lse, cos, sin, dqkv, kt, dk, dv):
    kt[...] = k[...].astype(F32).T.astype(BF16)
    for step in range(4):
        at = slice(step * 256, (step + 1) * 256)
        qb, dmb = q[at, :], dm[at, :]
        s = masked(dot_nt(k[...], qb), step, info[16])
        p = jnp.exp2(s * (SCALE * LOG2E) - lse[j : j + 1, at])
        more = dot(p.astype(BF16), dmb)
        dv[...] = more if step == 0 else dv[...] + more
        delta = jnp.sum((dmb.astype(F32) * mixed[at, :].astype(F32)).T, axis=0, keepdims=True)
        ds = (p * (dot_nt(v[...], dmb) - delta)).astype(BF16)
        more = dot(ds, qb)
        dk[...] = more if step == 0 else dk[...] + more
        dq = dot(kt[...], ds).T * SCALE
        dqkv[at, :HD] = (dq * cos[at, :] - half_turn(dq) * sin[at, :]).astype(BF16)
    u = dk[...] * SCALE
    dqkv[:, HD : 2 * HD] = (u * cos[...] - half_turn(u) * sin[...]).astype(BF16)
    dqkv[:, 2 * HD :] = dv[...].astype(BF16)


def to_places(full, i, rows):
    half = PART // 2
    for p in range(4):
        for g in range(2):
            top = p * 2 * PART + g * half
            to = i * 640 + (p * 2 + g) * PART
            rows[to : to + PART, :] = jnp.concatenate(
                [full[top : top + half], full[top + PART : top + PART + half]], axis=0
            ).astype(BF16)


def pick_y(info, rows, outs):
    for j in range(4):
        for m in range(4):
            at = pl.ds(pl.multiple_of(info[32 + j * 4 + m], 16), PART)
            outs[j][m * PART : (m + 1) * PART, :] = rows[at, :]


def pick_x(info, rows, outs):
    for j in range(4):
        for m in range(4):
            at = pl.ds(pl.multiple_of(info[32 + j * 4 + m], 16), PART)
            outs[m][j * PART : (j + 1) * PART, :] = rows[at, :]


def head_loads(j, far, near, sems):
    col = slice(j * HD, (j + 1) * HD)
    return [
        pltpu.make_async_copy(a.at[:, col], b, sems.at[i])
        for i, (a, b) in enumerate(zip(far, near))
    ]


def attn_bwd_kernel(info, *refs):
    ds = refs[:8]
    wo_far, k_far, q_far, v_far, mixed_far, h1_far, w_far, cos, sin, lse = refs[8:18]
    outs = refs[18:22]
    dqkv, dm1, gain = refs[22:25]
    k, q, v, wo, mixed, h1, w, da, dm0, kt, dk, dv, rows, sems = refs[25:]
    loads = [
        pltpu.make_async_copy(wo_far, wo, sems.at[3]),
        pltpu.make_async_copy(mixed_far, mixed, sems.at[4]),
        pltpu.make_async_copy(h1_far, h1, sems.at[5]),
        pltpu.make_async_copy(w_far.at[:, :SLOT], w, sems.at[6]),
    ]
    loads[0].start()
    heads = head_loads(0, (k_far, q_far, v_far), (k, q, v), sems)
    for load in heads + loads[1:]:
        load.start()
    for i in range(8):
        da[rows_of(info[i] * ROWS), :] = ds[i][...]
    loads[0].wait()

    @pl.loop(0, 4)
    def _(step):
        at = rows_of(step * 256, 256)
        dmix = dot(da[at, :], wo[...]).astype(BF16)
        dm0[at, :] = dmix[:, :HD]
        dm1[at, :] = dmix[:, HD:]

    for load in heads + loads[1:2]:
        load.wait()
    slot_bwd(0, info, k, q, v, dm0, mixed.at[:, :HD], lse, cos, sin, dqkv, kt, dk, dv)
    for load in loads[2:]:
        load.wait()
    for i in range(2):
        cut = slice(i * 640, (i + 1) * 640)
        dw = dot_tn(h1[:, cut], dqkv[...])
        gain[cut, :] = jnp.sum(dw * w[cut, :].astype(F32), axis=1, keepdims=True)
        do = dot_tn(da[:, cut], mixed[...])
        to_places(jnp.concatenate([dw, do], axis=1), i, rows)
    pick_y(info, rows, outs)


def attn_bwd_second_kernel(info, *refs):
    dm, k_far, q_far, v_far, mixed_far, h1_far, w_far, cos, sin, lse, gain, sums = refs[:12]
    outs = refs[12:16]
    dqkv = refs[16]
    k, q, v, mixed, h1, w, kt, dk, dv, rows, sems = refs[17:]
    loads = [
        pltpu.make_async_copy(h1_far, h1, sems.at[5]),
        pltpu.make_async_copy(w_far.at[:, SLOT:], w, sems.at[6]),
    ]
    heads = head_loads(1, (k_far, q_far, v_far, mixed_far), (k, q, v, mixed), sems)
    for load in heads + loads:
        load.start()
    for load in heads:
        load.wait()
    slot_bwd(1, info, k, q, v, dm, mixed, lse, cos, sin, dqkv, kt, dk, dv)
    for load in loads:
        load.wait()
    for i in range(2):
        cut = slice(i * 640, (i + 1) * 640)
        dw = dot_tn(h1[:, cut], dqkv[...])
        both = gain[cut, :] + jnp.sum(dw * w[cut, :SLOT].astype(F32), axis=1, keepdims=True)
        extra = sums[:, cut].T
        lane = lax.broadcasted_iota(jnp.int32, extra.shape, 1)
        extra = jnp.where(lane == 0, both / w[cut, SLOT : SLOT + 1].astype(F32), extra)
        to_places(jnp.concatenate([dw, extra], axis=1), i, rows)
    pick_x(info, rows, outs)


def attn_in_kernel(info, *refs):
    w, dq0, dq1, a, b, part = refs

    @pl.loop(0, 4)
    def _(step):
        at = rows_of(step * 256, 256)
        both = jnp.concatenate([dq0[at, :], dq1[at, :]], axis=1)
        part[at, :] = dot_nt(both, w[:, :QKV]).astype(BF16)

    give_blocks(info, part, a, b)


def finish_kernel(info, dw, qkv, out, gains, router, loss):
    for g in range(GROUPS):
        for j in range(SLOTS):
            for part in range(3):
                to = part * D + g * HW + j * HD
                at = j * SPLIT_A + part * HD
                qkv[:, to : to + HD] = dw[g, :, at : at + HD].astype(F32)
        out[:, g * HW : (g + 1) * HW] = dw[g, :, SLOT:SPLIT_A].astype(F32)
    last = slice(SPLIT_A + SLOT, WA)
    total = dw[0, :, last].astype(F32)
    for g in range(1, 8):
        total = total + dw[g, :, last].astype(F32)
    router[...] = total[:, 2:5]
    loss[...] = total[0:1, 5:6]
    gains[...] = total.T[0:8, :]


def call(kernel, info, args, outs, scratch, flops, mib, far_in=(), far_out=(), sems=0):
    total = sum(int(np.prod(x.shape)) * x.dtype.itemsize for x in args)
    total += sum(int(np.prod(s)) * jnp.dtype(t).itemsize for s, t in outs)

    def spec(far):
        return pl.BlockSpec(memory_space=pltpu.HBM if far else pltpu.VMEM)

    return pl.pallas_call(
        kernel,
        out_shape=[jax.ShapeDtypeStruct(s, t) for s, t in outs],
        in_specs=[pl.BlockSpec(memory_space=pltpu.SMEM)]
        + [spec(i in far_in) for i in range(len(args))],
        out_specs=[spec(i in far_out) for i in range(len(outs))],
        scratch_shapes=[pltpu.VMEM(s, t) for s, t in scratch]
        + ([pltpu.SemaphoreType.DMA((sems,))] if sems else []),
        compiler_params=pltpu.CompilerParams(vmem_limit_bytes=mib * MIB),
        cost_estimate=pl.CostEstimate(flops=flops, bytes_accessed=total, transcendentals=0),
    )(info, *args)


def exchange(x):
    return lax.ppermute(x, ("c", "xh"), [(0, 0), (1, 2), (2, 1), (3, 3)])


def turn_out(x):
    pairs = [(i * 4 + j * 2 + k, j * 4 + k * 2 + i) for i in (0, 1) for j in (0, 1) for k in (0, 1)]
    return lax.ppermute(x, ("xl", "c", "xh"), pairs)


def turn_home(x):
    pairs = [(j * 4 + k * 2 + i, i * 4 + j * 2 + k) for i in (0, 1) for j in (0, 1) for k in (0, 1)]
    return lax.ppermute(x, ("xl", "c", "xh"), pairs)


def along_z(x, k):
    return lax.ppermute(x, "z", [(i, (i + k) % 4) for i in range(4)])


def along_y(x, k):
    return lax.ppermute(x, "y", [(i, (i + k) % 4) for i in range(4)])


def along_x(x, k):
    place = [0, 2, 1, 3]
    return lax.ppermute(x, ("xl", "xh"), [(place[i], place[(i + k) % 4]) for i in range(4)])


def after(x, *deps):
    return lax.optimization_barrier((x, deps))[0]


def add_parts(parts, move):
    total = parts[0].astype(F32)
    for k in (1, 2, 3):
        total = total + move(parts[k], k).astype(F32)
    return total.astype(BF16)


def to_other_core(x):
    return lax.ppermute(x, "c", [(0, 1), (1, 0)])


def gather_group(x, *deps):
    own = [x] + [along_z(x, k) for k in (1, 2, 3)]
    last = after(own[3], *deps) if deps else own[3]
    return own + [to_other_core(part) for part in own[:3] + [last]]


def scatter_group(a, b):
    got = to_other_core(b)
    s = [
        (a[i * ROWS : (i + 1) * ROWS].astype(F32) + got[i * ROWS : (i + 1) * ROWS].astype(F32))
        for i in range(4)
    ]
    total = s[0]
    for k in (1, 2, 3):
        total = total + along_z(s[k].astype(BF16), k).astype(F32)
    return total


def sum_cores(a, b):
    got = to_other_core(b)
    cuts = [slice(k * ROWS, (k + 1) * ROWS) for k in range(4)]
    return [(a[cut].astype(F32) + got[cut].astype(F32)).astype(BF16) for cut in cuts]


def scatter_home(parts):
    total = 0.0
    for k in range(4):
        pairs = [
            (c * 8 + x * 4 + z, x * 8 + c * 4 + (z + k) % 4)
            for c in range(2)
            for x in range(2)
            for z in range(4)
        ]
        total = total + lax.ppermute(parts[k], ("c", "xh", "z"), pairs).astype(F32)
    return total


PLANE = ("y", "xl", "xh")
RING = ("y", "xh", "xl")


def rope_tables():
    places = jnp.arange(SEQ, dtype=jnp.int32).astype(F32)
    half = HD // 2
    speeds = rope_base ** (-jnp.arange(half, dtype=F32) / half)
    angles = places[:, None] * speeds[None, :]
    c, s = jnp.cos(angles), jnp.sin(angles)
    return jnp.concatenate([c, c], axis=1), jnp.concatenate([-s, s], axis=1)


def on_device(
    tokens, teacher, prefix, routes, attn_gain, w_qkv, w_out, router_w, ffn_gain, w_gate_up, w_down
):
    core, zz = lax.axis_index("c"), lax.axis_index("z")
    near = [core * 4 + (zz + k) % 4 for k in range(4)]
    far = [(1 - core) * 4 + (zz + k) % 4 for k in range(4)]
    back = [0, 3, 2, 1]
    sequence = lax.axis_index(PLANE)
    yy = lax.axis_index("y")
    xx = lax.axis_index("xh") * 2 + lax.axis_index("xl")

    def place(dy, dx):
        y, x = (yy + dy) % 4, (xx + dx) % 4
        return (y * 4 + x % 2 * 2 + x // 2) * PART

    info = jnp.stack(
        [near[i] for i in back]
        + [far[i] for i in back]
        + near
        + far
        + [prefix[sequence]]
        + [jnp.int32(0)] * 15
        + [place(j, m) for j in range(4) for m in range(4)]
    ).astype(jnp.int32)

    lanes = jnp.arange(EXT, dtype=jnp.int32)[None, :]
    chosen = (routes[:, 0:1] + 2 == lanes) | (routes[:, 1:2] + 2 == lanes)
    x_all = exchange(jnp.concatenate([tokens, chosen.astype(BF16)], axis=1))
    small = jnp.concatenate([attn_gain[:, None], ffn_gain[:, None], router_w], axis=1)
    raw = jnp.concatenate([w_qkv, w_out, jnp.pad(small, ((0, 0), (0, EXT - 5)))], axis=1)
    n = raw.shape[0]
    heads = raw[:, : 3 * D].reshape(n, 3, GROUPS, SLOTS, HD).transpose(2, 0, 3, 1, 4)
    outs = raw[:, 3 * D : 4 * D].reshape(n, GROUPS, HW).transpose(1, 0, 2)
    extra = jnp.broadcast_to(raw[None, :, 4 * D :], (8, n, EXT))
    none = ((0, 8 - GROUPS), (0, 0), (0, 0))
    packed = jnp.concatenate(
        [jnp.pad(heads.reshape(GROUPS, n, QKV), none), extra, jnp.pad(outs, none)], axis=2
    )
    packed = lax.all_to_all(packed, ("c", "z"), split_axis=0, concat_axis=0).reshape(8 * n, WA)
    lane_pad = 128 - UNITS
    wm_own = jnp.concatenate(
        [
            jnp.pad(w_gate_up, ((0, 0), (0, 0), (0, 0), (0, lane_pad))).reshape(-1, GU),
            jnp.pad(w_down, ((0, 0), (0, 0), (0, lane_pad))).reshape(-1, DN),
        ],
        axis=1,
    )
    wm_own = turn_out(wm_own)
    w_all = lax.all_gather(packed, RING, axis=0, tiled=True)
    x_seq, chosen_all = call(
        place_kernel,
        info,
        gather_group(x_all),
        [((SEQ, D), BF16), ((SEQ, EXT), BF16)],
        [],
        0,
        6,
    )
    cos, sin = rope_tables()
    wm = lax.all_gather(after(wm_own, w_all, x_seq, cos, sin), RING, axis=0, tiled=True)
    teach = exchange(teacher)

    head = ((SEQ, HW), BF16)
    w, h1, q, k, v, mixed, wo, a, b, wext, lse, ext = call(
        attn_fwd_kernel,
        info,
        [w_all, x_seq, cos, sin],
        [
            ((D, WQ), BF16),
            ((SEQ, D), BF16),
            head,
            head,
            head,
            head,
            ((D, HW), BF16),
            ((512, D), BF16),
            ((512, D), BF16),
            ((D, EXT), BF16),
            ((8, SEQ), F32),
            ((EXT, D), F32),
        ],
        [
            ((D, WQ), BF16),
            ((SEQ, D), BF16),
            head,
            head,
            head,
            head,
            ((D, HW), BF16),
            ((D, WA), BF16),
            ((HW, SEQ), BF16),
            ((SEQ, D), BF16),
        ],
        5_000_000_000,
        LIM[0],
        far_in=(0,),
        far_out=range(7),
        sems=8,
    )
    x = x_all[:, :D].astype(F32)
    x1 = x + scatter_group(a, b)
    r2 = lax.rsqrt(jnp.mean(x1 * x1, axis=1, keepdims=True) + norm_eps)
    n2 = x1 * r2
    gain_two = ext[1:2, :]
    h2 = (n2 * gain_two).astype(BF16)

    a, b, h2_all, gu, z, comb = call(
        moe_fwd_kernel,
        info,
        gather_group(h2, wm) + [wm, wext, chosen_all],
        [
            ((512, D), BF16),
            ((512, D), BF16),
            ((SEQ, D), BF16),
            ((SEQ, GU), F32),
            ((SEQ, DN), BF16),
            ((SEQ, EXT), F32),
        ],
        [((SEQ, D), BF16)],
        4_000_000_000,
        LIM[2],
    )
    y = x1 + scatter_group(a, b)
    diff = y - teach.astype(F32)
    squares = jnp.sum(diff * diff)
    dm = diff.astype(BF16)
    a, b, dm_all, dgu = call(
        moe_bwd_kernel,
        info,
        gather_group(dm) + [wm, gu, comb],
        [((512, D + EXT), BF16), ((512, D + EXT), BF16), ((SEQ, D), BF16), ((SEQ, GU), BF16)],
        [((SEQ, D + EXT), BF16)],
        4_000_000_000,
        LIM[3],
    )
    (dwm,) = call(
        moe_grad_kernel,
        info,
        [h2_all, dgu, dm_all, z],
        [((D, WM), BF16)],
        [((D, WM), BF16)],
        4_000_000_000,
        LIM[4],
        far_out=(0,),
        sems=2,
    )
    dwm_own = lax.psum_scatter(dwm, RING, scatter_dimension=0, tiled=True)
    dh2 = scatter_group(a, b)
    dcomb = dh2[:, D + 2 : D + 5] + dh2[:, D + 5 : D + 8]
    router = ext[2:5, :].astype(BF16)
    logits = lax.dot_general(h2, router, NT, preferred_element_type=F32)
    gates = jax.nn.softmax(logits, axis=1)
    dpick = dcomb * x_all[:, D + 2 : D + 5].astype(F32)
    dlogits = (gates * (dpick - jnp.sum(dpick * gates, axis=1, keepdims=True))).astype(BF16)
    d_router = lax.dot_general(dlogits, h2, TN, preferred_element_type=F32)
    dh2 = dh2[:, :D] + jnp.dot(dlogits, router, preferred_element_type=F32)
    d_ffn_gain = jnp.sum(dh2 * n2, axis=0, keepdims=True)
    g2 = dh2 * gain_two
    dx1 = diff + r2 * (g2 - n2 * jnp.mean(g2 * n2, axis=1, keepdims=True))
    da = dx1.astype(BF16)
    da_home = exchange(da)
    y_home = exchange(y.astype(BF16))

    sums = jnp.concatenate(
        [
            jnp.zeros((1, D), F32),
            d_ffn_gain,
            d_router,
            jnp.full((1, D), squares / (SEQ * 16), F32),
        ],
        axis=0,
    )
    sums = jnp.pad(sums, ((0, EXT - 6), (0, 0)))
    one = ((SEQ, HD), BF16)
    *a_blocks, dq0, dm1, gain = call(
        attn_bwd_kernel,
        info,
        gather_group(da)
        + [wo, k, q, v, mixed, h1, w, cos, sin, after(lse, da_home, y_home)],
        [((4 * PART, SPLIT_A), BF16)] * 4 + [((SEQ, SLOT), BF16), one, ((D, 1), F32)],
        [
            one,
            one,
            one,
            ((D, HW), BF16),
            head,
            ((SEQ, D), BF16),
            ((D, SLOT), BF16),
            ((SEQ, D), BF16),
            one,
            ((HD, SEQ), BF16),
            ((SEQ, HD), F32),
            ((SEQ, HD), F32),
            ((D, SPLIT_A), BF16),
        ],
        5_000_000_000,
        LIM[5],
        far_in=range(8, 15),
        sems=7,
    )
    *b_blocks, dq1 = call(
        attn_bwd_second_kernel,
        info,
        [dm1, k, q, v, mixed, h1, w, cos, sin, lse, gain, sums],
        [((4 * PART, WA - SPLIT_A), BF16)] * 4 + [((SEQ, SLOT), BF16)],
        [
            one,
            one,
            one,
            one,
            ((SEQ, D), BF16),
            ((D, SLOT + EXT), BF16),
            ((HD, SEQ), BF16),
            ((SEQ, HD), F32),
            ((SEQ, HD), F32),
            ((D, WA - SPLIT_A), BF16),
        ],
        3_000_000_000,
        LIM[7],
        far_in=range(1, 7),
        sems=7,
    )
    a, b = call(
        attn_in_kernel,
        info,
        [w, dq0, dq1],
        [((512, D), BF16), ((512, D), BF16)],
        [((SEQ, D), BF16)],
        2_000_000_000,
        LIM[6],
    )
    x = tokens.astype(F32)
    to_z = sum_cores(a, b)
    first = (
        add_parts([after(a_blocks[0], to_z)] + a_blocks[1:], along_y),
        add_parts([after(b_blocks[0], to_z)] + b_blocks[1:], along_x),
    )
    dwm_own = turn_home(after(dwm_own, first))
    cuts = [slice(i * PART, (i + 1) * PART) for i in range(4)]
    dw = jnp.concatenate(
        [
            add_parts([first[0][cut] for cut in cuts], along_x),
            add_parts([first[1][cut] for cut in cuts], along_y),
        ],
        axis=1,
    )
    dh1 = scatter_home(to_z)
    dw = lax.all_to_all(dw.reshape(8, n, WA), ("c", "z"), split_axis=0, concat_axis=0)
    dw = after(dw, dwm_own)
    d_qkv, d_out, d_gains, d_router, loss = call(
        finish_kernel,
        info,
        [dw],
        [((n, 3 * D), F32), ((n, D), F32), ((8, n), F32), ((n, 3), F32), ((1, 1), F32)],
        [],
        0,
        6,
    )

    r1 = lax.rsqrt(jnp.mean(x * x, axis=1, keepdims=True) + norm_eps)
    n1 = x * r1
    g1 = dh1 * ext[0:1, :]
    d_tokens = da_home.astype(F32) + r1 * (g1 - n1 * jnp.mean(g1 * n1, axis=1, keepdims=True))

    d_gu = dwm_own[:, :GU].reshape(-1, 4, 2, 128)[..., :UNITS].astype(F32)
    d_dn = dwm_own[:, GU:].reshape(-1, 4, 128)[..., :UNITS].astype(F32)
    return (
        y_home,
        loss.reshape(()),
        d_tokens,
        d_gains[0],
        d_qkv,
        d_out,
        d_router,
        d_gains[1],
        d_gu,
        d_dn,
    )


def solution(mesh):
    fine = Mesh(mesh.devices.reshape(4, 2, 2, 2, 4), ("y", "xl", "c", "xh", "z"))
    every = ("y", "xl", "c", "xh", "z")
    rows = P(every, None)
    in_specs = (
        rows,
        rows,
        P(),
        rows,
        P(every),
        rows,
        rows,
        rows,
        P(every),
        P(("y", "xl", "c"), None, None, ("xh", "z")),
        P(("y", "xl", "c"), None, ("xh", "z")),
    )
    out_specs = (
        rows,
        P(),
        rows,
        P(every),
        rows,
        rows,
        rows,
        P(every),
        P(("y", "xl", "c"), None, None, ("xh", "z")),
        P(("y", "xl", "c"), None, ("xh", "z")),
    )
    return jax.shard_map(
        on_device, mesh=fine, in_specs=in_specs, out_specs=out_specs, check_vma=False
    )
```
